128 devices in a mesh: xy: 32 (over x, y, core), gz: 4 (over z).
Axes of the slice: x: 4, y: 4, z: 4, core: 2. Of those that a mesh axis runs over, the one named last changes fastest.
Arguments:
- estimate: float32 [512, 64, 512], P('xy', None, 'gz'), may hold values from 0.25 to 4
- observed: float32 [6, 512, 64, 512], P(None, None, 'xy', 'gz'), may hold values from 0.2 to 5
- kernels: float32 [6, 3, 15], replicated, may hold values from 0.05 to 1
- view_shift: int32 [6], replicated, may hold values from -16 to 16
Outputs:
- updated: float32 [512, 64, 512], P('xy', None, 'gz')
The draws below stay inside these ranges and needn't reach their ends.
All inputs are finite; a program needn't handle non-finite values.
Results may differ from the reference program's by a relative error of at most 0.0001.
Values sent between devices are 32-bit elements; how exact they have to be, the bound alone decides.
A program may use at most 128 MiB of HBM per device.

```python
import math
import jax
import jax.numpy as jnp
from jax import lax

NY = 64
VIEWS = 6
TAPS = 15
MAX_SHIFT = 16
NX = 512
NZ = 512


def plant(entries, own_key, least, largest):
    longest = entries.shape.index(max(entries.shape))
    spots = []
    for shift in (0, 1):
        where = [jax.random.randint(jax.random.fold_in(own_key, axis), (), 0, length) for axis, length in enumerate(entries.shape)]
        where[longest] = (where[longest] + shift) % entries.shape[longest]
        spots.append(tuple(where))
    return entries.at[spots[0]].set(least).at[spots[1]].set(largest)


def block_scale(rng, dims, cuts, low, top_value):
    level = 1.0
    for axis_at, blocks in cuts:
        draws = jax.random.uniform(jax.random.fold_in(jax.random.fold_in(rng, 6), axis_at), (blocks,), jnp.float32, low / len(cuts), top_value / len(cuts))
        level = level * jnp.repeat(jnp.exp(draws), dims[axis_at] // blocks).reshape((-1,) + (1,) * (len(dims) - 1 - axis_at))
    return level


def setup_inputs(seed: int = 0) -> dict:
    key_of = jax.random.split(jax.random.key(seed), 5)
    estimate = jnp.clip(jnp.exp(math.log(4.0) - 2.7725887 * jax.random.uniform(key_of[0], (NX, NY, NZ), jnp.float32) ** block_scale(key_of[0], (NX, NY, NZ), ((0, 32), (2, 4)), -0.2, 0.2)), 0.25, 4.0)
    observed = jnp.clip(jnp.exp(math.log(5.0) - 3.218876 * jax.random.uniform(key_of[1], (VIEWS, NX, NY, NZ), jnp.float32) ** block_scale(key_of[1], (VIEWS, NX, NY, NZ), ((2, 32), (3, 4)), -0.2, 0.2)), 0.2, 5.0)
    kernels = jnp.clip(jnp.exp(jax.random.uniform(key_of[2], (VIEWS, 3, TAPS), jnp.float32, math.log(0.05), math.log(1.0))), 0.05, 1.0)
    view_shift = plant(jax.random.randint(key_of[3], (VIEWS,), 0 - MAX_SHIFT, MAX_SHIFT + 1), jax.random.fold_in(key_of[3], 1), 0 - MAX_SHIFT, MAX_SHIFT).astype(jnp.int32)
    return dict(estimate=estimate, observed=observed, kernels=kernels, view_shift=view_shift)


def correlate(field, kernel, dim_pos):
    half_width = kernel.shape[0] // 2
    amount = field.shape[dim_pos]
    widths = [(0, 0)] * field.ndim
    widths[dim_pos] = (half_width, half_width)
    padded = jnp.pad(field, widths)
    result = jnp.zeros_like(field)
    for step in range(kernel.shape[0]):
        result = result + kernel[step] * lax.slice_in_dim(padded, step, step + amount, axis=dim_pos)
    return result


def blur_three(field, factors):
    result = correlate(field, factors[0], 0)
    result = correlate(result, factors[1], 1)
    return correlate(result, factors[2], 2)


def reference(estimate, observed, kernels, view_shift):
    kernel_norm = kernels / jnp.sum(kernels, axis=2, keepdims=True)
    flipped = kernel_norm[:, :, ::-1]
    rows_y = observed.shape[2]

    def one_view(view, back_sum):
        factors = kernel_norm[view]
        blurred = blur_three(estimate, factors)
        offset = view_shift[view]
        padded = jnp.pad(observed[view], ((0, 0), (MAX_SHIFT, MAX_SHIFT), (0, 0)))
        aligned = lax.dynamic_slice_in_dim(padded, (MAX_SHIFT + offset).astype(jnp.int32), rows_y, axis=1)
        places = jnp.arange(rows_y, dtype=jnp.int32) + offset
        covered = ((places >= 0) & (places < rows_y))[None, :, None]
        ratio = jnp.where(covered, aligned / blurred, jnp.float32(1.0))
        return back_sum + blur_three(ratio, flipped[view])

    back_sum = lax.fori_loop(0, VIEWS, one_view, jnp.zeros_like(estimate))
    return estimate * back_sum / VIEWS
```

```python
import functools

import jax
import jax.numpy as jnp
from jax import lax
from jax.experimental import pallas as pl
from jax.experimental.pallas import tpu as pltpu
from jax.sharding import PartitionSpec as P

MESH = pl.DeviceIdType.MESH
F32, BF16 = jnp.float32, jnp.bfloat16
TAPS, HALF = 15, 7
SIDES = ((-1, 0), (1, 0), (0, -1), (0, 1), (-1, -1), (-1, 1), (1, -1), (1, 1))


def split(a):
    high = a.astype(BF16)
    return high, (a - high.astype(F32)).astype(BF16)


def dot3(a, b, dims):
    (ah, al), (bh, bl) = a, b
    one = lambda p, q: lax.dot_general(p, q, (dims, ((), ())), preferred_element_type=F32)
    return one(ah, bh) + (one(al, bh) + one(ah, bl))


NN = ((1,), (0,))
NT = ((1,), (1,))
TN = ((0,), (0,))


def kernel(n, depth, views, taps_ref, shift_ref, est_ref, obs_ref, out_ref, *scratch):
    tiles = scratch[:views]
    (field, halo_z, zed, xed, blurs, ratio, yed, spread, total, spill, got_x, got_z,
     w_main, w_back, w_side,
     a2a_send, a2a_recv, own_sem, halo_send, halo_recv, spill_send, spill_recv) = scratch[views:]
    rows = 2 * n
    slab = rows * 8
    me, deep = lax.axis_index("xy"), lax.axis_index("gz")

    def peer(side):
        return {"xy": lax.rem(me + side[0] + n, n), "gz": lax.rem(deep + side[1] + depth, depth)}

    barrier = pltpu.get_barrier_semaphore()

    def greet(k, carry):
        pl.semaphore_signal(barrier, inc=1, device_id={"xy": lax.rem(me + k, n)}, device_id_type=MESH)
        return carry

    lax.fori_loop(1, n, greet, 0)
    for side in SIDES[2:]:
        pl.semaphore_signal(barrier, inc=1, device_id=peer(side), device_id_type=MESH)

    def arrange(y, carry):
        for t in range(2):
            field[1 + t, y] = est_ref[pl.ds(t * 8 * rows + y, 8, stride=rows), :]
        return carry

    lax.fori_loop(0, rows, arrange, 0)
    for t in range(2):
        turned = field[1 + t].reshape(slab, 128).T
        spill[0, 1 + t] = turned[0:8]
        spill[1, 1 + t] = turned[120:128]
    pl.semaphore_wait(barrier, n - 1 + 6)

    def halo_copies():
        out = []
        for i, (sx, sz) in enumerate(SIDES):
            if sz == 0:
                src = field.at[1 if sx < 0 else 2]
                dst = field.at[3 if sx < 0 else 0]
            else:
                mine, theirs = (0, 1) if sz < 0 else (1, 0)
                if sx == 0:
                    src, dst = spill.at[mine, pl.ds(1, 2)], halo_z.at[theirs, pl.ds(1, 2)]
                else:
                    src = spill.at[mine, 1 if sx < 0 else 2]
                    dst = halo_z.at[theirs, 3 if sx < 0 else 0]
            out.append(pltpu.make_async_remote_copy(
                src_ref=src, dst_ref=dst, send_sem=halo_send.at[i], recv_sem=halo_recv.at[i],
                device_id=peer((sx, sz)), device_id_type=MESH))
        return out

    halos = halo_copies()
    for copy in halos:
        copy.start()

    for v in range(views):
        def send(k, carry, v=v):
            to = lax.rem(me + k, n)
            pltpu.make_async_remote_copy(
                src_ref=obs_ref.at[v, pl.ds(pl.multiple_of(to * 32, 32), 32)],
                dst_ref=tiles[v].at[me],
                send_sem=a2a_send.at[v], recv_sem=a2a_recv.at[v],
                device_id={"xy": to}, device_id_type=MESH).start()
            return carry

        lax.fori_loop(1, n, send, 0)
        pltpu.make_async_copy(
            obs_ref.at[v, pl.ds(pl.multiple_of(me * 32, 32), 32)], tiles[v].at[me], own_sem.at[v]).start()

    def tap(v, axis, t):
        return taps_ref[(v * 3 + axis) * TAPS + t]

    def banded(v, tap_at):
        band = jnp.zeros(tap_at.shape, F32)
        for t in range(TAPS):
            band = jnp.where(tap_at == t, tap(v, 2, t), band)
        return band

    def build(v, carry):
        row = lax.broadcasted_iota(jnp.int32, (128, 128), 0)
        col = lax.broadcasted_iota(jnp.int32, (128, 128), 1)
        w_main[v, 0], w_main[v, 1] = split(banded(v, row - col + HALF))
        w_back[v, 0], w_back[v, 1] = split(banded(v, col - row + HALF))
        row = lax.broadcasted_iota(jnp.int32, (16, 128), 0)
        col = lax.broadcasted_iota(jnp.int32, (16, 128), 1)
        place = jnp.where(row < 8, row - 8, row + 120)
        w_side[v, 0], w_side[v, 1] = split(banded(v, place - col + HALF))
        return carry

    lax.fori_loop(0, views, build, 0)
    xed[0:8] = jnp.zeros((8, 16, 128), F32)
    xed[rows + 8:rows + 16] = jnp.zeros((8, 16, 128), F32)
    ratio[0:8] = jnp.zeros((8, 16, 128), F32)
    ratio[rows + 8:rows + 16] = jnp.zeros((8, 16, 128), F32)
    yed[:, 0:8] = jnp.zeros((rows, 8, 128), F32)
    yed[:, 24:32] = jnp.zeros((rows, 8, 128), F32)

    for copy in halos:
        copy.wait_recv()
    first, last = me == 0, me == n - 1
    front, rear = deep == 0, deep == depth - 1
    field[0] = jnp.where(first, 0.0, field[0])
    field[3] = jnp.where(last, 0.0, field[3])
    halo_z[0] = jnp.where(front, 0.0, halo_z[0])
    halo_z[1] = jnp.where(rear, 0.0, halo_z[1])
    for side in range(2):
        halo_z[side, 0] = jnp.where(first, 0.0, halo_z[side, 0])
        halo_z[side, 3] = jnp.where(last, 0.0, halo_z[side, 3])

    def along_y(taps, src, put):
        def block(b, carry):
            for t in range(2):
                sums = [None] * 8
                for r in range(22):
                    seen = src[b * 8 + 1 + r, pl.ds(t * 8, 8), :]
                    for j in range(max(0, r - 14), min(8, r + 1)):
                        term = taps[r - j] * seen
                        sums[j] = term if sums[j] is None else sums[j] + term
                for j in range(8):
                    put(b * 8 + j, t, sums[j])
            return carry

        lax.fori_loop(0, rows // 8, block, 0)

    def forward(v, carry):
        main, side = (w_main[v, 0], w_main[v, 1]), (w_side[v, 0], w_side[v, 1])
        for t in range(4):
            res = dot3(split(field[t].reshape(slab, 128)), main, NN)
            ends = jnp.concatenate([halo_z[0, t], halo_z[1, t]], axis=0)
            res = res + dot3(split(ends), side, TN)
            zed[:, t * 8:t * 8 + 8, :] = res.reshape(rows, 8, 128)
        taps = [jnp.full((8, 128), tap(v, 0, t), F32) for t in range(TAPS)]

        def along_x(y, c):
            low = high = None
            for o in range(1, 24):
                seen = zed[y, pl.ds(o, 8), :]
                if o <= 15:
                    term = taps[o - 1] * seen
                    low = term if low is None else low + term
                if o >= 9:
                    term = taps[o - 9] * seen
                    high = term if high is None else high + term
            xed[y + 8, 0:8, :] = low
            xed[y + 8, 8:16, :] = high
            return c

        lax.fori_loop(0, rows, along_x, 0, unroll=4)
        taps_y = [jnp.full((8, 128), tap(v, 1, t), F32) for t in range(TAPS)]

        def put(y, t, value):
            blurs[v, y, pl.ds(t * 8, 8), :] = value

        along_y(taps_y, xed, put)
        return carry

    lax.fori_loop(0, views, forward, 0)

    def backward(v):
        shift = shift_ref[v]
        whole = tiles[v].at[pl.ds(0, n - 1)]
        pltpu.make_async_copy(whole, whole, a2a_recv.at[v]).wait()
        pltpu.make_async_copy(
            obs_ref.at[v, pl.ds(pl.multiple_of(me * 32, 32), 32)], tiles[v].at[me], own_sem.at[v]).wait()
        flat = tiles[v].reshape(n * 32, 128)

        def divide(y, carry):
            at = y + shift
            inside = jnp.clip(at, 0, rows - 1)
            base = (inside // 2) * 32 + inside % 2
            covered = jnp.logical_and(at >= 0, at < rows)
            for t in range(2):
                seen = flat[pl.ds(base + t * 16, 8, stride=2), :]
                ratio[y + 8, pl.ds(t * 8, 8), :] = jnp.where(
                    covered, seen / blurs[v, y, pl.ds(t * 8, 8), :], jnp.float32(1.0))
            return carry

        lax.fori_loop(0, rows, divide, 0, unroll=4)
        taps_y = [jnp.full((8, 128), tap(v, 1, TAPS - 1 - t), F32) for t in range(TAPS)]

        def put(y, t, value):
            yed[y, pl.ds(8 + t * 8, 8), :] = value

        along_y(taps_y, ratio, put)
        taps = [jnp.full((8, 128), tap(v, 0, TAPS - 1 - t), F32) for t in range(TAPS)]

        def along_x(y, c):
            sums = [None] * 4
            for o in range(1, 24):
                seen = yed[y, pl.ds(o, 8), :]
                for j in range(4):
                    t = o + 7 - 8 * j
                    if 0 <= t < TAPS:
                        term = taps[t] * seen
                        sums[j] = term if sums[j] is None else sums[j] + term
            for j in range(4):
                spread[j, y] = sums[j]
            return c

        lax.fori_loop(0, rows, along_x, 0, unroll=2)
        main, side = (w_back[v, 0], w_back[v, 1]), (w_side[v, 0], w_side[v, 1])
        for t in range(4):
            parts = split(spread[t].reshape(slab, 128))
            res = dot3(parts, main, NN).reshape(rows, 8, 128)
            ends = dot3(side, parts, NT)
            if v == 0:
                total[t] = res
                spill[0, t], spill[1, t] = ends[0:8], ends[8:16]
            else:
                total[t] += res
                spill[0, t] += ends[0:8]
                spill[1, t] += ends[8:16]

    for copy in halos:
        copy.wait_send()
    for v in range(views):
        backward(v)

    spills = []
    for i, (sx, sz) in enumerate(SIDES):
        if sz == 0:
            src, dst = total.at[0 if sx < 0 else 3], got_x.at[1 if sx < 0 else 0]
        else:
            mine, theirs = (0, 1) if sz < 0 else (1, 0)
            if sx == 0:
                src, dst = spill.at[mine, pl.ds(1, 2)], got_z.at[theirs, pl.ds(1, 2)]
            else:
                src = spill.at[mine, 0 if sx < 0 else 3]
                dst = got_z.at[theirs, 3 if sx < 0 else 0]
        spills.append(pltpu.make_async_remote_copy(
            src_ref=src, dst_ref=dst, send_sem=spill_send.at[i], recv_sem=spill_recv.at[i],
            device_id=peer((sx, sz)), device_id_type=MESH))
    for copy in spills:
        copy.start()
    for v in range(views):
        whole = tiles[v].at[pl.ds(0, n - 1)]
        pltpu.make_async_copy(whole, whole, a2a_send.at[v]).wait()
    for copy in spills:
        copy.wait_recv()

    lane = lax.broadcasted_iota(jnp.int32, (16, 128), 1)
    row = lax.broadcasted_iota(jnp.int32, (16, 128), 0)
    place = jnp.where(lane == jnp.where(row < 8, row, row + 112), 1.0, 0.0).astype(BF16)
    for t in range(2):
        outer, edge = (0, first) if t == 0 else (1, last)
        corner = 0 if t == 0 else 3
        ends = []
        for side, face in ((0, front), (1, rear)):
            end = got_z[side, 1 + t] + jnp.where(edge, 0.0, got_z[side, corner])
            ends.append(jnp.where(face, 0.0, end))
        eh, el = split(jnp.concatenate(ends, axis=0))
        one = lambda p: lax.dot_general(p, place, (TN, ((), ())), preferred_element_type=F32)
        spilled = (one(eh) + one(el)).reshape(rows, 8, 128)
        summed = total[1 + t] + jnp.where(edge, 0.0, got_x[outer]) + spilled
        spread[t] = field[1 + t] * summed / views

    def finish(y, carry):
        for t in range(2):
            out_ref[pl.ds(t * 8 * rows + y, 8, stride=rows), :] = spread[t, y]
        return carry

    lax.fori_loop(0, rows, finish, 0)
    for copy in spills:
        copy.wait_send()


def local(n, depth, estimate, observed, kernels, view_shift):
    views, nx = observed.shape[:2]
    rows = estimate.shape[1]
    taps = (kernels / jnp.sum(kernels, axis=2, keepdims=True)).reshape(-1)
    est = estimate.reshape(16 * rows, 128)
    obs = observed.reshape(views, 2 * nx, 128)
    dma = pltpu.SemaphoreType.DMA
    vmem = lambda *shape: pltpu.VMEM(shape, F32)
    wide = lambda *shape: pltpu.VMEM(shape, BF16)
    out = pl.pallas_call(
        functools.partial(kernel, n, depth, views),
        out_shape=jax.ShapeDtypeStruct((16 * rows, 128), F32),
        in_specs=[
            pl.BlockSpec(memory_space=pltpu.SMEM),
            pl.BlockSpec(memory_space=pltpu.SMEM),
            pl.BlockSpec(memory_space=pltpu.VMEM),
            pl.BlockSpec(memory_space=pl.ANY),
        ],
        out_specs=pl.BlockSpec(memory_space=pltpu.VMEM),
        scratch_shapes=[vmem(n, 32, 128)] * views + [
            vmem(4, rows, 8, 128),
            vmem(2, 4, 8, rows * 8),
            vmem(rows, 32, 128),
            vmem(rows + 16, 16, 128),
            vmem(views, rows, 16, 128),
            vmem(rows + 16, 16, 128),
            vmem(rows, 32, 128),
            vmem(4, rows, 8, 128),
            vmem(4, rows, 8, 128),
            vmem(2, 4, 8, rows * 8),
            vmem(2, rows, 8, 128),
            vmem(2, 4, 8, rows * 8),
            wide(views, 2, 128, 128),
            wide(views, 2, 128, 128),
            wide(views, 2, 16, 128),
            dma((views,)), dma((views,)), dma((views,)),
            dma((8,)), dma((8,)), dma((8,)), dma((8,)),
        ],
        compiler_params=pltpu.CompilerParams(
            collective_id=0, has_side_effects=True, vmem_limit_bytes=56 * 2**20),
    )(taps, view_shift, est, obs)
    return out.reshape(estimate.shape)


def solution(mesh):
    return jax.shard_map(
        functools.partial(local, mesh.shape["xy"], mesh.shape["gz"]),
        mesh=mesh,
        in_specs=(P("xy", None, "gz"), P(None, None, "xy", "gz"), P(), P()),
        out_specs=P("xy", None, "gz"),
        check_vma=False,
    )
```

```python
import functools

import jax
import jax.numpy as jnp
from jax import lax
from jax.experimental import pallas as pl
from jax.experimental.pallas import tpu as pltpu
from jax.sharding import PartitionSpec as P

MESH = pl.DeviceIdType.MESH
F32, BF16 = jnp.float32, jnp.bfloat16
TAPS, HALF = 15, 7
SIDES = ((-1, 0), (1, 0), (0, -1), (0, 1), (-1, -1), (-1, 1), (1, -1), (1, 1))


def split(a):
    high = a.astype(BF16)
    return high, (a - high.astype(F32)).astype(BF16)


def dot(a, b, dims):
    return lax.dot_general(a, b, (dims, ((), ())), preferred_element_type=F32)


NN = ((1,), (0,))
NT = ((1,), (1,))
TN = ((0,), (0,))
CHUNK = 16


def kernel(n, depth, views, kernels_ref, shift_ref, est_ref, obs_ref, out_ref,
           est, tiles, lined, field, wide, halo_z, zed, xed, weights, ratio, yed, spread, total, spill,
           got_x, got_z, w_fore, w_back, w_low, w_side,
           est_sem, a2a_send, a2a_recv, own_sem, halo_send, halo_recv, spill_send, spill_recv,
           chunk_send, chunk_recv):
    rows = 2 * n
    slab = rows * 8
    chunks = rows // CHUNK
    me, deep = lax.axis_index("xy"), lax.axis_index("gz")
    load = pltpu.make_async_copy(est_ref, est, est_sem)
    load.start()

    def peer(side):
        return {"xy": lax.rem(me + side[0] + n, n), "gz": lax.rem(deep + side[1] + depth, depth)}

    barrier = pltpu.get_barrier_semaphore()

    def greet(k, carry):
        pl.semaphore_signal(barrier, inc=1, device_id={"xy": lax.rem(me + k, n)}, device_id_type=MESH)
        return carry

    lax.fori_loop(1, n, greet, 0)
    for side in SIDES[2:]:
        pl.semaphore_signal(barrier, inc=1, device_id=peer(side), device_id_type=MESH)

    def own(v, wait):
        copy = pltpu.make_async_copy(
            obs_ref.at[v, pl.ds(pl.multiple_of(me * 32, 32), 32)], tiles.at[v, me], own_sem.at[v])
        copy.wait() if wait else copy.start()

    for v in range(views):
        own(v, False)

    load.wait()

    def arrange(y, carry):
        for t in range(2):
            field[1 + t, y] = est[pl.ds(t * 8 * rows + y, 8, stride=rows), :]
        return carry

    lax.fori_loop(0, rows, arrange, 0, unroll=8)
    for t in range(2):
        turned = field[1 + t].reshape(slab, 128).T
        spill[0, 1 + t] = turned[0:8]
        spill[1, 1 + t] = turned[120:128]
    pl.semaphore_wait(barrier, n - 1 + 6)

    halos = []
    for i, (sx, sz) in enumerate(SIDES):
        if sz == 0:
            src = field.at[1 if sx < 0 else 2]
            dst = field.at[3 if sx < 0 else 0]
        else:
            mine, theirs = (0, 1) if sz < 0 else (1, 0)
            if sx == 0:
                src, dst = spill.at[mine, pl.ds(1, 2)], halo_z.at[theirs, pl.ds(1, 2)]
            else:
                src = spill.at[mine, 1 if sx < 0 else 2]
                dst = halo_z.at[theirs, 3 if sx < 0 else 0]
        halos.append(pltpu.make_async_remote_copy(
            src_ref=src, dst_ref=dst, send_sem=halo_send.at[i], recv_sem=halo_recv.at[i],
            device_id=peer((sx, sz)), device_id_type=MESH))
    for copy in halos:
        copy.start()

    def send(v, k):
        to = lax.rem(me + k, n)
        pltpu.make_async_remote_copy(
            src_ref=obs_ref.at[v, pl.ds(pl.multiple_of(to * 32, 32), 32)],
            dst_ref=tiles.at[v, me],
            send_sem=a2a_send.at[v], recv_sem=a2a_recv.at[v],
            device_id={"xy": to}, device_id_type=MESH).start()

    def send_first(k, carry):
        send(0, k)
        return carry

    lax.fori_loop(1, n, send_first, 0)

    def paced(group, body, steps):
        if group is None:
            lax.fori_loop(0, steps, lambda i, c: (body(i), c)[1], 0)
            return
        v, half = 1 + lax.div(group, 2), lax.rem(group, 2)
        each = n // 2
        if steps < each:
            def many(i, c):
                for j in range(each):
                    @pl.when(1 + half * each + j < n)
                    def _():
                        send(v, 1 + half * each + j)
                return c
            lax.fori_loop(0, 1, many, 0)
            lax.fori_loop(0, steps, lambda i, c: (body(i), c)[1], 0)
            return

        def step(i, c):
            send(v, 1 + half * each + i)
            body(i)
            return c

        lax.fori_loop(0, each - 1, step, 0)

        @pl.when(half == 0)
        def _():
            send(v, each)

        lax.fori_loop(each - 1, steps, lambda i, c: (body(i), c)[1], 0)

    def taps_of(v, axis, flip):
        raw = [jnp.full((8, 128), kernels_ref[v, axis, t], F32) for t in range(TAPS)]
        whole = raw[0]
        for t in range(1, TAPS):
            whole = whole + raw[t]
        scale = 1.0 / whole
        taps = [r * scale for r in raw]
        return taps[::-1] if flip else taps

    def build(v, carry):
        raw = [kernels_ref[v, 2, t] for t in range(TAPS)]
        whole = jnp.full((1, 128), raw[0], F32)
        for t in range(1, TAPS):
            whole = whole + raw[t]
        scale = 1.0 / whole

        def banded(tap_at):
            band = jnp.zeros(tap_at.shape, F32)
            for t in range(TAPS):
                band = jnp.where(tap_at == t, raw[t], band)
            return split(band * scale)

        pair, lanes = lax.div(v, 2), pl.ds(pl.multiple_of(lax.rem(v, 2) * 128, 128), 128)
        row = lax.broadcasted_iota(jnp.int32, (128, 128), 0)
        col = lax.broadcasted_iota(jnp.int32, (128, 128), 1)
        high, low = banded(row - col + HALF)
        w_fore[pair, 0:128, lanes] = high
        w_fore[pair, 128:256, lanes] = high
        w_fore[pair, 256:384, lanes] = low
        high, low = banded(col - row + HALF)
        w_back[v, 0:128] = high
        w_back[v, 128:256] = high
        w_low[v] = low
        row = lax.broadcasted_iota(jnp.int32, (16, 128), 0)
        col = lax.broadcasted_iota(jnp.int32, (16, 128), 1)
        high, low = banded(jnp.where(row < 8, row - 8, row + 120) - col + HALF)
        w_side[v, 0:16] = high
        w_side[v, 16:32] = low
        w_fore[pair, 384:400, lanes] = high
        w_fore[pair, 400:416, lanes] = high
        w_fore[pair, 416:432, lanes] = low
        w_fore[pair, 432:512, lanes] = jnp.zeros((80, 128), BF16)
        return carry

    lax.fori_loop(0, views, build, 0)
    xed[0:8] = jnp.zeros((8, 16, 128), F32)
    xed[rows + 8:rows + 16] = jnp.zeros((8, 16, 128), F32)
    ratio[0:8] = jnp.zeros((8, 16, 128), F32)
    ratio[rows + 8:rows + 16] = jnp.zeros((8, 16, 128), F32)
    lined[0:16] = jnp.ones((16, 16, 128), F32)
    lined[rows + 16:rows + 32] = jnp.ones((16, 16, 128), F32)
    yed[:, 0:8] = jnp.zeros((rows, 8, 128), F32)
    yed[:, 24:32] = jnp.zeros((rows, 8, 128), F32)

    first, last = me == 0, me == n - 1
    front, rear = deep == 0, deep == depth - 1

    def widen(t, gone):
        high, low = split(jnp.where(gone, 0.0, field[t].reshape(slab, 128)))
        ends = []
        for side, face in ((0, front), (1, rear)):
            ends.append(jnp.where(jnp.logical_or(gone, face), 0.0, halo_z[side, t]))
        eh, el = split(jnp.concatenate(ends, axis=0))
        eh, el = eh.astype(F32), el.astype(F32)
        ends = jnp.concatenate([eh, el, eh, jnp.zeros((80, slab), F32)], axis=0).T
        wide[t, :, 0:128] = high
        wide[t, :, 128:256] = low
        wide[t, :, 256:384] = high
        wide[t, :, 384:512] = ends.astype(BF16)

    for copy in halos:
        copy.wait_recv()
    for t, gone in enumerate((first, False, False, last)):
        widen(t, gone)

    def along_y(taps, src, put, blocks):
        def block(b, carry):
            for t in range(2):
                sums = [None] * 8
                for r in range(22):
                    seen = src[b * 8 + 1 + r, pl.ds(t * 8, 8), :]
                    for j in range(max(0, r - 14), min(8, r + 1)):
                        term = taps[r - j] * seen
                        sums[j] = term if sums[j] is None else sums[j] + term
                for j in range(8):
                    put(b * 8 + j, t, sums[j])
            return carry

        lax.fori_loop(*blocks, block, 0)

    def forward(v, carry):
        part = lax.rem(v, 2)

        @pl.when(part == 0)
        def _():
            pair = lax.div(v, 2)

            def tile(t, c):
                res = dot(wide[t], w_fore[pair], NN)
                for p in range(2):
                    zed[p, :, pl.ds(pl.multiple_of(t * 8, 8), 8), :] = res[:, p * 128:p * 128 + 128].reshape(rows, 8, 128)
                return c

            lax.fori_loop(0, 4, tile, 0)

        taps = taps_of(v, 0, False)

        def along_x(i):
            for q in range(4):
                y = i * 4 + q
                low = high = None
                for o in range(1, 24):
                    seen = zed[part, y, pl.ds(o, 8), :]
                    if o <= 15:
                        term = taps[o - 1] * seen
                        low = term if low is None else low + term
                    if o >= 9:
                        term = taps[o - 9] * seen
                        high = term if high is None else high + term
                xed[y + 8, 0:8, :] = low
                xed[y + 8, 8:16, :] = high

        paced(v, along_x, rows // 4)

        def put(y, t, value):
            near = pl.reciprocal(value, approx=True)
            weights[v, y, pl.ds(t * 8, 8), :] = near * (2.0 - value * near)

        along_y(taps_of(v, 1, False), xed, put, (0, rows // 8))
        return carry

    lax.fori_loop(0, views, forward, 0)

    for copy in halos:
        copy.wait_send()

    def spill_chunk(c, side):
        at = pl.ds(pl.multiple_of(c * CHUNK, CHUNK), CHUNK)
        src, dst = total.at[0 if side == 0 else 3, at], got_x.at[1 - side, at]
        return pltpu.make_async_remote_copy(
            src_ref=src, dst_ref=dst, send_sem=chunk_send.at[side, c], recv_sem=chunk_recv.at[side, c],
            device_id=peer(SIDES[side]), device_id_type=MESH)

    def backward(v, group, final):
        shift = shift_ref[v]
        whole = tiles.at[v, pl.ds(0, n - 1)]
        pltpu.make_async_copy(whole, whole, a2a_recv.at[v]).wait()
        own(v, True)

        def line(d, c):
            for p in range(2):
                for t in range(2):
                    lined[16 + d * 2 + p, pl.ds(t * 8, 8), :] = tiles[v, d, pl.ds(p + t * 16, 8, stride=2), :]
            return c

        lax.fori_loop(0, n, line, 0, unroll=4)

        def divide(y, c):
            at = y + shift
            covered = jnp.logical_and(at >= 0, at < rows)
            ratio[y + 8] = jnp.where(covered, lined[at + 16] * weights[v, y], jnp.float32(1.0))
            return c

        lax.fori_loop(0, rows, divide, 0, unroll=8)

        def put(y, t, value):
            yed[y, pl.ds(8 + t * 8, 8), :] = value

        def along_x(taps, y, to):
            sums = [None] * 4
            for o in range(1, 24):
                seen = yed[y, pl.ds(o, 8), :]
                for j in range(4):
                    t = o + 7 - 8 * j
                    if 0 <= t < TAPS:
                        term = taps[t] * seen
                        sums[j] = term if sums[j] is None else sums[j] + term
            for j in range(4):
                spread[j, to] = sums[j]

        def finish_chunk(c):
            at = pl.ds(pl.multiple_of(c * CHUNK, CHUNK), CHUNK)
            lanes = pl.ds(pl.multiple_of(c * CHUNK * 8, CHUNK * 8), CHUNK * 8)
            src = spread[:, at] if not final else spread[:, 0:CHUNK]
            high, low = split(src.reshape(4 * CHUNK * 8, 128))
            res = dot(jnp.concatenate([high, low], axis=1), w_back[v], NN) + dot(high, w_low[v], NN)
            res = res.reshape(4, CHUNK, 8, 128)
            ends = dot(w_side[v], high, NT)
            ends = ends[0:16] + ends[16:32] + dot(w_side[v, 0:16], low, NT)
            for t in range(4):
                total[t, at] += res[t]
                for side in range(2):
                    spill[side, t, :, lanes] += ends[side * 8:side * 8 + 8, t * CHUNK * 8:(t + 1) * CHUNK * 8]

        if not final:
            along_y(taps_of(v, 1, True), ratio, put, (0, rows // 8))
            taps = taps_of(v, 0, True)

            def step(i):
                for q in range(4):
                    along_x(taps, i * 4 + q, i * 4 + q)

            paced(group, step, rows // 4)
            lax.fori_loop(0, chunks, lambda c, k: (finish_chunk(c), k)[1], 0)
            return

        def chunk(c, k):
            along_y(taps_of(v, 1, True), ratio, put, (c * (CHUNK // 8), (c + 1) * (CHUNK // 8)))
            taps = taps_of(v, 0, True)

            def step(i, kk):
                for q in range(4):
                    along_x(taps, c * CHUNK + i * 4 + q, i * 4 + q)
                return kk

            lax.fori_loop(0, CHUNK // 4, step, 0)
            finish_chunk(c)
            for side in range(2):
                spill_chunk(c, side).start()
            return k

        lax.fori_loop(0, chunks, chunk, 0)

    for t in range(4):
        total[t] = jnp.zeros((rows, 8, 128), F32)
        spill[0, t] = jnp.zeros((8, slab), F32)
        spill[1, t] = jnp.zeros((8, slab), F32)
    with_sends = 2 * (views - 1) - views
    lax.fori_loop(0, with_sends, lambda v, c: (backward(v, v + views, False), c)[1], 0)
    lax.fori_loop(with_sends, views - 1, lambda v, c: (backward(v, None, False), c)[1], 0)
    backward(views - 1, None, True)

    spills = []
    for i, (sx, sz) in enumerate(SIDES[2:]):
        mine, theirs = (0, 1) if sz < 0 else (1, 0)
        if sx == 0:
            src, dst = spill.at[mine, pl.ds(1, 2)], got_z.at[theirs, pl.ds(1, 2)]
        else:
            src = spill.at[mine, 0 if sx < 0 else 3]
            dst = got_z.at[theirs, 3 if sx < 0 else 0]
        spills.append(pltpu.make_async_remote_copy(
            src_ref=src, dst_ref=dst, send_sem=spill_send.at[i], recv_sem=spill_recv.at[i],
            device_id=peer((sx, sz)), device_id_type=MESH))
    for copy in spills:
        copy.start()
    for v in range(views):
        whole = tiles.at[v, pl.ds(0, n - 1)]
        pltpu.make_async_copy(whole, whole, a2a_send.at[v]).wait()
    for copy in spills:
        copy.wait_recv()

    lane = lax.broadcasted_iota(jnp.int32, (32, 128), 1)
    row = lax.broadcasted_iota(jnp.int32, (32, 128), 0) % 16
    place = jnp.where(lane == jnp.where(row < 8, row, row + 112), 1.0, 0.0).astype(BF16)

    def last_chunk(c, k):
        at = pl.ds(pl.multiple_of(c * CHUNK, CHUNK), CHUNK)
        lanes = pl.ds(pl.multiple_of(c * CHUNK * 8, CHUNK * 8), CHUNK * 8)
        for side in range(2):
            spill_chunk(c, side).wait_recv()
        for t in range(2):
            outer, edge = (0, first) if t == 0 else (1, last)
            corner = 0 if t == 0 else 3
            ends = []
            for side, face in ((0, front), (1, rear)):
                end = got_z[side, 1 + t, :, lanes] + jnp.where(edge, 0.0, got_z[side, corner, :, lanes])
                ends.append(jnp.where(face, 0.0, end))
            both = jnp.concatenate(split(jnp.concatenate(ends, axis=0)), axis=0)
            spilled = dot(both, place, TN).reshape(CHUNK, 8, 128)
            summed = total[1 + t, at] + jnp.where(edge, 0.0, got_x[outer, at]) + spilled
            done = field[1 + t, at] * (summed * (1.0 / views))
            for q in range(CHUNK):
                out_ref[pl.ds(t * 8 * rows + c * CHUNK + q, 8, stride=rows), :] = done[q]
        return k

    lax.fori_loop(0, chunks, last_chunk, 0)
    for copy in spills:
        copy.wait_send()
    for c in range(chunks):
        for side in range(2):
            spill_chunk(c, side).wait_send()


def local(n, depth, estimate, observed, kernels, view_shift):
    views, nx = observed.shape[:2]
    rows = estimate.shape[1]
    est = estimate.reshape(16 * rows, 128)
    obs = observed.reshape(views, 2 * nx, 128)
    dma = pltpu.SemaphoreType.DMA
    vmem = lambda *shape: pltpu.VMEM(shape, F32)
    half = lambda *shape: pltpu.VMEM(shape, BF16)
    out = pl.pallas_call(
        functools.partial(kernel, n, depth, views),
        out_shape=jax.ShapeDtypeStruct((16 * rows, 128), F32),
        in_specs=[
            pl.BlockSpec(memory_space=pltpu.SMEM),
            pl.BlockSpec(memory_space=pltpu.SMEM),
            pl.BlockSpec(memory_space=pl.ANY),
            pl.BlockSpec(memory_space=pl.ANY),
        ],
        out_specs=pl.BlockSpec(memory_space=pltpu.VMEM),
        scratch_shapes=[
            vmem(16 * rows, 128),
            vmem(views, n, 32, 128),
            vmem(rows + 32, 16, 128),
            vmem(4, rows, 8, 128),
            half(4, rows * 8, 512),
            vmem(2, 4, 8, rows * 8),
            vmem(2, rows, 32, 128),
            vmem(rows + 16, 16, 128),
            vmem(views, rows, 16, 128),
            vmem(rows + 16, 16, 128),
            vmem(rows, 32, 128),
            vmem(4, rows, 8, 128),
            vmem(4, rows, 8, 128),
            vmem(2, 4, 8, rows * 8),
            vmem(2, rows, 8, 128),
            vmem(2, 4, 8, rows * 8),
            half(views // 2, 512, 256),
            half(views, 256, 128),
            half(views, 128, 128),
            half(views, 32, 128),
            dma(()), dma((views,)), dma((views,)), dma((views,)),
            dma((8,)), dma((8,)), dma((6,)), dma((6,)),
            dma((2, rows // CHUNK)), dma((2, rows // CHUNK)),
        ],
        compiler_params=pltpu.CompilerParams(
            collective_id=0, has_side_effects=True, vmem_limit_bytes=56 * 2**20),
    )(kernels, view_shift, est, obs)
    return out.reshape(estimate.shape)


def solution(mesh):
    return jax.shard_map(
        functools.partial(local, mesh.shape["xy"], mesh.shape["gz"]),
        mesh=mesh,
        in_specs=(P("xy", None, "gz"), P(None, None, "xy", "gz"), P(), P()),
        out_specs=P("xy", None, "gz"),
        check_vma=False,
    )
```

```python
import functools

import jax
import jax.numpy as jnp
from jax import lax
from jax.experimental import pallas as pl
from jax.experimental.pallas import tpu as pltpu
from jax.sharding import PartitionSpec as P

MESH = pl.DeviceIdType.MESH
F32, BF16 = jnp.float32, jnp.bfloat16
TAPS, HALF = 15, 7
SIDES = ((-1, 0), (1, 0), (0, -1), (0, 1), (-1, -1), (-1, 1), (1, -1), (1, 1))


def split(a):
    high = a.astype(BF16)
    return high, (a - high.astype(F32)).astype(BF16)


def dot(a, b, dims):
    return lax.dot_general(a, b, (dims, ((), ())), preferred_element_type=F32)


NN = ((1,), (0,))
NT = ((1,), (1,))
TN = ((0,), (0,))
CHUNK = 16
STEPS = 8
EARLY = 2


def kernel(n, depth, views, kernels_ref, shift_ref, est_ref, obs_ref, out_ref,
           est, tiles, lined, field, wide, halo_z, zed, xed, weights, ratio, yed, spread, total, spill,
           got_x, got_z, w_fore, w_back, w_low, w_side,
           est_sem, a2a_send, a2a_recv, own_sem, halo_send, halo_recv, spill_send, spill_recv,
           chunk_send, chunk_recv):
    rows = 2 * n
    slab = rows * 8
    chunks = rows // CHUNK
    me, deep = lax.axis_index("xy"), lax.axis_index("gz")
    load = pltpu.make_async_copy(est_ref, est, est_sem)
    load.start()

    def peer(side):
        return {"xy": lax.rem(me + side[0] + n, n), "gz": lax.rem(deep + side[1] + depth, depth)}

    barrier = pltpu.get_barrier_semaphore()

    def greet(k, carry):
        pl.semaphore_signal(barrier, inc=1, device_id={"xy": lax.rem(me + k, n)}, device_id_type=MESH)
        return carry

    lax.fori_loop(1, n, greet, 0)
    for side in SIDES[2:]:
        pl.semaphore_signal(barrier, inc=1, device_id=peer(side), device_id_type=MESH)

    def own(v, wait):
        copy = pltpu.make_async_copy(
            obs_ref.at[v, pl.ds(pl.multiple_of(me * 32, 32), 32)], tiles.at[v, me], own_sem.at[v])
        copy.wait() if wait else copy.start()

    for v in range(views):
        own(v, False)

    load.wait()

    def arrange(y, carry):
        for t in range(2):
            field[1 + t, y] = est[pl.ds(t * 8 * rows + y, 8, stride=rows), :]
        return carry

    lax.fori_loop(0, rows, arrange, 0, unroll=8)
    for t in range(2):
        turned = field[1 + t].reshape(slab, 128).T
        spill[0, 1 + t] = turned[0:8]
        spill[1, 1 + t] = turned[120:128]
    pl.semaphore_wait(barrier, n - 1 + 6)

    halos = []
    for i, (sx, sz) in enumerate(SIDES):
        if sz == 0:
            src = field.at[1 if sx < 0 else 2]
            dst = field.at[3 if sx < 0 else 0]
        else:
            mine, theirs = (0, 1) if sz < 0 else (1, 0)
            if sx == 0:
                src, dst = spill.at[mine, pl.ds(1, 2)], halo_z.at[theirs, pl.ds(1, 2)]
            else:
                src = spill.at[mine, 1 if sx < 0 else 2]
                dst = halo_z.at[theirs, 3 if sx < 0 else 0]
        halos.append(pltpu.make_async_remote_copy(
            src_ref=src, dst_ref=dst, send_sem=halo_send.at[i], recv_sem=halo_recv.at[i],
            device_id=peer((sx, sz)), device_id_type=MESH))
    for copy in halos:
        copy.start()

    def send(v, i):
        to = lax.rem(me + 1 + lax.rem(i * 13, n - 1), n)
        pltpu.make_async_remote_copy(
            src_ref=obs_ref.at[v, pl.ds(pl.multiple_of(to * 32, 32), 32)],
            dst_ref=tiles.at[v, me],
            send_sem=a2a_send.at[v], recv_sem=a2a_recv.at[v],
            device_id={"xy": to}, device_id_type=MESH).start()

    lax.fori_loop(0, n - 1, lambda i, c: (send(0, i), c)[1], 0)

    def paced(group, body):
        if group is None:
            lax.fori_loop(0, STEPS, lambda i, c: (body(i), c)[1], 0)
            return
        v, half = EARLY + lax.div(group, 2), lax.rem(group, 2)
        each = n // 2
        per = each // STEPS

        def step(i, c):
            for j in range(per):
                send(v, half * each + i * per + j)
            body(i)
            return c

        lax.fori_loop(0, STEPS - 1, step, 0)
        for j in range(per - 1):
            send(v, half * each + (STEPS - 1) * per + j)

        @pl.when(half == 0)
        def _():
            send(v, each - 1)

        body(STEPS - 1)

    def taps_of(v, axis, flip):
        raw = [jnp.full((8, 128), kernels_ref[v, axis, t], F32) for t in range(TAPS)]
        whole = raw[0]
        for t in range(1, TAPS):
            whole = whole + raw[t]
        scale = 1.0 / whole
        taps = [r * scale for r in raw]
        return taps[::-1] if flip else taps

    def build(v, carry):
        raw = [kernels_ref[v, 2, t] for t in range(TAPS)]
        whole = jnp.full((1, 128), raw[0], F32)
        for t in range(1, TAPS):
            whole = whole + raw[t]
        scale = 1.0 / whole

        def banded(tap_at):
            band = jnp.zeros(tap_at.shape, F32)
            for t in range(TAPS):
                band = jnp.where(tap_at == t, raw[t], band)
            return split(band * scale)

        pair, lanes = lax.div(v, 2), pl.ds(pl.multiple_of(lax.rem(v, 2) * 128, 128), 128)
        row = lax.broadcasted_iota(jnp.int32, (128, 128), 0)
        col = lax.broadcasted_iota(jnp.int32, (128, 128), 1)
        high, low = banded(row - col + HALF)
        w_fore[pair, 0:128, lanes] = high
        w_fore[pair, 128:256, lanes] = high
        w_fore[pair, 256:384, lanes] = low
        high, low = banded(col - row + HALF)
        w_back[v, 0:128] = high
        w_back[v, 128:256] = high
        w_low[v] = low
        row = lax.broadcasted_iota(jnp.int32, (16, 128), 0)
        col = lax.broadcasted_iota(jnp.int32, (16, 128), 1)
        high, low = banded(jnp.where(row < 8, row - 8, row + 120) - col + HALF)
        w_side[v, 0:16] = high
        w_side[v, 16:32] = low
        w_fore[pair, 384:400, lanes] = high
        w_fore[pair, 400:416, lanes] = high
        w_fore[pair, 416:432, lanes] = low
        w_fore[pair, 432:512, lanes] = jnp.zeros((80, 128), BF16)
        return carry

    lax.fori_loop(0, views, build, 0)
    xed[0:8] = jnp.zeros((8, 16, 128), F32)
    xed[rows + 8:rows + 16] = jnp.zeros((8, 16, 128), F32)
    ratio[0:8] = jnp.zeros((8, 16, 128), F32)
    ratio[rows + 8:rows + 16] = jnp.zeros((8, 16, 128), F32)
    lined[0:16] = jnp.ones((16, 16, 128), F32)
    lined[rows + 16:rows + 32] = jnp.ones((16, 16, 128), F32)
    yed[:, 0:8] = jnp.zeros((rows, 8, 128), F32)
    yed[:, 24:32] = jnp.zeros((rows, 8, 128), F32)

    first, last = me == 0, me == n - 1
    front, rear = deep == 0, deep == depth - 1

    def widen(t, gone):
        high, low = split(jnp.where(gone, 0.0, field[t].reshape(slab, 128)))
        ends = []
        for side, face in ((0, front), (1, rear)):
            ends.append(jnp.where(jnp.logical_or(gone, face), 0.0, halo_z[side, t]))
        eh, el = split(jnp.concatenate(ends, axis=0))
        eh, el = eh.astype(F32), el.astype(F32)
        ends = jnp.concatenate([eh, el, eh, jnp.zeros((80, slab), F32)], axis=0).T
        wide[t, :, 0:128] = high
        wide[t, :, 128:256] = low
        wide[t, :, 256:384] = high
        wide[t, :, 384:512] = ends.astype(BF16)

    for copy in halos:
        copy.wait_recv()
    lax.fori_loop(0, n - 1, lambda i, c: (send(1, i), c)[1], 0)
    for t, gone in enumerate((first, False, False, last)):
        widen(t, gone)

    def along_y(taps, src, put, blocks):
        def block(b, carry):
            for t in range(2):
                sums = [None] * 8
                for r in range(22):
                    seen = src[b * 8 + 1 + r, pl.ds(t * 8, 8), :]
                    for j in range(max(0, r - 14), min(8, r + 1)):
                        term = taps[r - j] * seen
                        sums[j] = term if sums[j] is None else sums[j] + term
                for j in range(8):
                    put(b * 8 + j, t, sums[j])
            return carry

        lax.fori_loop(*blocks, block, 0)

    def forward(v, carry):
        part = lax.rem(v, 2)

        @pl.when(part == 0)
        def _():
            pair = lax.div(v, 2)

            for t in range(4):
                res = dot(wide[t], w_fore[pair], NN)
                for p in range(2):
                    zed[p, :, t * 8:t * 8 + 8, :] = res[:, p * 128:p * 128 + 128].reshape(rows, 8, 128)

        taps = taps_of(v, 0, False)

        def along_x(i):
            for q in range(rows // STEPS):
                y = i * (rows // STEPS) + q
                low = high = None
                for o in range(1, 24):
                    seen = zed[part, y, pl.ds(o, 8), :]
                    if o <= 15:
                        term = taps[o - 1] * seen
                        low = term if low is None else low + term
                    if o >= 9:
                        term = taps[o - 9] * seen
                        high = term if high is None else high + term
                xed[y + 8, 0:8, :] = low
                xed[y + 8, 8:16, :] = high

        paced(v, along_x)

        def put(y, t, value):
            near = pl.reciprocal(value, approx=True)
            weights[v, y, pl.ds(t * 8, 8), :] = near * (2.0 - value * near)

        along_y(taps_of(v, 1, False), xed, put, (0, rows // 8))
        return carry

    lax.fori_loop(0, views, forward, 0)

    for copy in halos:
        copy.wait_send()

    def spill_chunk(c, side):
        at = pl.ds(pl.multiple_of(c * CHUNK, CHUNK), CHUNK)
        src, dst = total.at[0 if side == 0 else 3, at], got_x.at[1 - side, at]
        return pltpu.make_async_remote_copy(
            src_ref=src, dst_ref=dst, send_sem=chunk_send.at[side, c], recv_sem=chunk_recv.at[side, c],
            device_id=peer(SIDES[side]), device_id_type=MESH)

    def backward(v, group, final):
        shift = shift_ref[v]
        whole = tiles.at[v, pl.ds(0, n - 1)]
        pltpu.make_async_copy(whole, whole, a2a_recv.at[v]).wait()
        own(v, True)

        def line(d, c):
            for p in range(2):
                for t in range(2):
                    lined[16 + d * 2 + p, pl.ds(t * 8, 8), :] = tiles[v, d, pl.ds(p + t * 16, 8, stride=2), :]
            return c

        lax.fori_loop(0, n, line, 0, unroll=4)

        def divide(y, c):
            at = y + shift
            covered = jnp.logical_and(at >= 0, at < rows)
            ratio[y + 8] = jnp.where(covered, lined[at + 16] * weights[v, y], jnp.float32(1.0))
            return c

        lax.fori_loop(0, rows, divide, 0, unroll=8)

        def put(y, t, value):
            yed[y, pl.ds(8 + t * 8, 8), :] = value

        def along_x(taps, y, to):
            sums = [None] * 4
            for o in range(1, 24):
                seen = yed[y, pl.ds(o, 8), :]
                for j in range(4):
                    t = o + 7 - 8 * j
                    if 0 <= t < TAPS:
                        term = taps[t] * seen
                        sums[j] = term if sums[j] is None else sums[j] + term
            for j in range(4):
                spread[j, to] = sums[j]

        def finish_chunk(c):
            at = pl.ds(pl.multiple_of(c * CHUNK, CHUNK), CHUNK)
            lanes = pl.ds(pl.multiple_of(c * CHUNK * 8, CHUNK * 8), CHUNK * 8)
            high, low = split(spread[:, 0:CHUNK].reshape(4 * CHUNK * 8, 128))
            res = dot(jnp.concatenate([high, low], axis=1), w_back[v], NN) + dot(high, w_low[v], NN)
            res = res.reshape(4, CHUNK, 8, 128)
            ends = dot(w_side[v], high, NT)
            ends = ends[0:16] + ends[16:32] + dot(w_side[v, 0:16], low, NT)
            for t in range(4):
                total[t, at] += res[t]
                for side in range(2):
                    spill[side, t, :, lanes] += ends[side * 8:side * 8 + 8, t * CHUNK * 8:(t + 1) * CHUNK * 8]

        def finish_tile(t):
            high, low = split(spread[t].reshape(slab, 128))
            res = dot(jnp.concatenate([high, low], axis=1), w_back[v], NN) + dot(high, w_low[v], NN)
            ends = dot(w_side[v], high, NT)
            ends = ends[0:16] + ends[16:32] + dot(w_side[v, 0:16], low, NT)
            total[t] += res.reshape(rows, 8, 128)
            for side in range(2):
                spill[side, t] += ends[side * 8:side * 8 + 8]

        if not final:
            along_y(taps_of(v, 1, True), ratio, put, (0, rows // 8))
            taps = taps_of(v, 0, True)

            def step(i):
                for q in range(rows // STEPS):
                    y = i * (rows // STEPS) + q
                    along_x(taps, y, y)

            paced(group, step)
            for t in range(4):
                finish_tile(t)
            return

        def chunk(c, k):
            along_y(taps_of(v, 1, True), ratio, put, (c * (CHUNK // 8), (c + 1) * (CHUNK // 8)))
            taps = taps_of(v, 0, True)

            def step(i, kk):
                for q in range(4):
                    along_x(taps, c * CHUNK + i * 4 + q, i * 4 + q)
                return kk

            lax.fori_loop(0, CHUNK // 4, step, 0)
            finish_chunk(c)
            for side in range(2):
                spill_chunk(c, side).start()
            return k

        lax.fori_loop(0, chunks, chunk, 0)

    for t in range(4):
        total[t] = jnp.zeros((rows, 8, 128), F32)
        spill[0, t] = jnp.zeros((8, slab), F32)
        spill[1, t] = jnp.zeros((8, slab), F32)
    with_sends = 2 * (views - EARLY) - views
    lax.fori_loop(0, with_sends, lambda v, c: (backward(v, v + views, False), c)[1], 0)
    lax.fori_loop(with_sends, views - 1, lambda v, c: (backward(v, None, False), c)[1], 0)
    backward(views - 1, None, True)

    spills = []
    for i, (sx, sz) in enumerate(SIDES[2:]):
        mine, theirs = (0, 1) if sz < 0 else (1, 0)
        if sx == 0:
            src, dst = spill.at[mine, pl.ds(1, 2)], got_z.at[theirs, pl.ds(1, 2)]
        else:
            src = spill.at[mine, 0 if sx < 0 else 3]
            dst = got_z.at[theirs, 3 if sx < 0 else 0]
        spills.append(pltpu.make_async_remote_copy(
            src_ref=src, dst_ref=dst, send_sem=spill_send.at[i], recv_sem=spill_recv.at[i],
            device_id=peer((sx, sz)), device_id_type=MESH))
    for copy in spills:
        copy.start()
    for v in range(views):
        whole = tiles.at[v, pl.ds(0, n - 1)]
        pltpu.make_async_copy(whole, whole, a2a_send.at[v]).wait()
    for copy in spills:
        copy.wait_recv()

    lane = lax.broadcasted_iota(jnp.int32, (32, 128), 1)
    row = lax.broadcasted_iota(jnp.int32, (32, 128), 0) % 16
    place = jnp.where(lane == jnp.where(row < 8, row, row + 112), 1.0, 0.0).astype(BF16)

    def last_chunk(c, k):
        at = pl.ds(pl.multiple_of(c * CHUNK, CHUNK), CHUNK)
        lanes = pl.ds(pl.multiple_of(c * CHUNK * 8, CHUNK * 8), CHUNK * 8)
        for side in range(2):
            spill_chunk(c, side).wait_recv()
        for t in range(2):
            outer, edge = (0, first) if t == 0 else (1, last)
            corner = 0 if t == 0 else 3
            ends = []
            for side, face in ((0, front), (1, rear)):
                end = got_z[side, 1 + t, :, lanes] + jnp.where(edge, 0.0, got_z[side, corner, :, lanes])
                ends.append(jnp.where(face, 0.0, end))
            both = jnp.concatenate(split(jnp.concatenate(ends, axis=0)), axis=0)
            spilled = dot(both, place, TN).reshape(CHUNK, 8, 128)
            summed = total[1 + t, at] + jnp.where(edge, 0.0, got_x[outer, at]) + spilled
            done = field[1 + t, at] * (summed * (1.0 / views))
            for q in range(CHUNK):
                out_ref[pl.ds(t * 8 * rows + c * CHUNK + q, 8, stride=rows), :] = done[q]
        return k

    lax.fori_loop(0, chunks, last_chunk, 0)
    for copy in spills:
        copy.wait_send()
    for c in range(chunks):
        for side in range(2):
            spill_chunk(c, side).wait_send()


def local(n, depth, estimate, observed, kernels, view_shift):
    views, nx = observed.shape[:2]
    rows = estimate.shape[1]
    est = estimate.reshape(16 * rows, 128)
    obs = observed.reshape(views, 2 * nx, 128)
    dma = pltpu.SemaphoreType.DMA
    vmem = lambda *shape: pltpu.VMEM(shape, F32)
    half = lambda *shape: pltpu.VMEM(shape, BF16)
    out = pl.pallas_call(
        functools.partial(kernel, n, depth, views),
        out_shape=pltpu.VMEM((16 * rows, 128), F32),
        in_specs=[
            pl.BlockSpec(memory_space=pltpu.SMEM),
            pl.BlockSpec(memory_space=pltpu.SMEM),
            pl.BlockSpec(memory_space=pl.ANY),
            pl.BlockSpec(memory_space=pl.ANY),
        ],
        out_specs=pl.BlockSpec(memory_space=pltpu.VMEM),
        scratch_shapes=[
            vmem(16 * rows, 128),
            vmem(views, n, 32, 128),
            vmem(rows + 32, 16, 128),
            vmem(4, rows, 8, 128),
            half(4, rows * 8, 512),
            vmem(2, 4, 8, rows * 8),
            vmem(2, rows, 32, 128),
            vmem(rows + 16, 16, 128),
            vmem(views, rows, 16, 128),
            vmem(rows + 16, 16, 128),
            vmem(rows, 32, 128),
            vmem(4, rows, 8, 128),
            vmem(4, rows, 8, 128),
            vmem(2, 4, 8, rows * 8),
            vmem(2, rows, 8, 128),
            vmem(2, 4, 8, rows * 8),
            half(views // 2, 512, 256),
            half(views, 256, 128),
            half(views, 128, 128),
            half(views, 32, 128),
            dma(()), dma((views,)), dma((views,)), dma((views,)),
            dma((8,)), dma((8,)), dma((6,)), dma((6,)),
            dma((2, rows // CHUNK)), dma((2, rows // CHUNK)),
        ],
        compiler_params=pltpu.CompilerParams(
            collective_id=0, has_side_effects=True, vmem_limit_bytes=56 * 2**20),
    )(kernels, view_shift, est, obs)
    return out.reshape(estimate.shape)


def solution(mesh):
    return jax.shard_map(
        functools.partial(local, mesh.shape["xy"], mesh.shape["gz"]),
        mesh=mesh,
        in_specs=(P("xy", None, "gz"), P(None, None, "xy", "gz"), P(), P()),
        out_specs=P("xy", None, "gz"),
        check_vma=False,
    )
```

```python
import functools

import jax
import jax.numpy as jnp
from jax import lax
from jax.experimental import pallas as pl
from jax.experimental.pallas import tpu as pltpu
from jax.sharding import PartitionSpec as P

MESH = pl.DeviceIdType.MESH
F32, BF16 = jnp.float32, jnp.bfloat16
TAPS, HALF = 15, 7
SIDES = ((-1, 0), (1, 0), (0, -1), (0, 1), (-1, -1), (-1, 1), (1, -1), (1, 1))


def split(a):
    high = a.astype(BF16)
    return high, (a - high.astype(F32)).astype(BF16)


def dot(a, b, dims):
    return lax.dot_general(a, b, (dims, ((), ())), preferred_element_type=F32)


NN = ((1,), (0,))
NT = ((1,), (1,))
TN = ((0,), (0,))
CHUNK = 16
STEPS = 8
EARLY = 2


def kernel(n, depth, views, kernels_in, shift_in, est_ref, obs_ref, out_ref,
           kernels_ref, shift_ref, small_sem, est, tiles, lined, field, wide, halo_z, zed, xed, weights, ratio, yed, spread, total, spill,
           got_x, got_z, w_fore, w_back, w_low, w_side,
           est_sem, a2a_send, a2a_recv, own_sem, halo_send, halo_recv, spill_send, spill_recv,
           chunk_send, chunk_recv):
    rows = 2 * n
    slab = rows * 8
    chunks = rows // CHUNK
    me, deep = lax.axis_index("xy"), lax.axis_index("gz")
    def peer(side):
        return {"xy": lax.rem(me + side[0] + n, n), "gz": lax.rem(deep + side[1] + depth, depth)}

    barrier = pltpu.get_barrier_semaphore()

    def greet(k, carry):
        pl.semaphore_signal(barrier, inc=1, device_id={"xy": lax.rem(me + k, n)}, device_id_type=MESH)
        return carry

    lax.fori_loop(1, n, greet, 0, unroll=31)
    for side in SIDES[2:]:
        pl.semaphore_signal(barrier, inc=1, device_id=peer(side), device_id_type=MESH)

    load = pltpu.make_async_copy(est_ref, est, est_sem)
    load.start()
    small = (pltpu.make_async_copy(kernels_in, kernels_ref, small_sem.at[0]),
             pltpu.make_async_copy(shift_in, shift_ref, small_sem.at[1]))
    for copy in small:
        copy.start()

    def own(v, wait):
        copy = pltpu.make_async_copy(
            obs_ref.at[v, pl.ds(pl.multiple_of(me * 32, 32), 32)], tiles.at[v, me], own_sem.at[v])
        copy.wait() if wait else copy.start()

    for v in range(views):
        own(v, False)

    load.wait()

    def arrange(y, carry):
        for t in range(2):
            field[1 + t, y] = est[pl.ds(t * 8 * rows + y, 8, stride=rows), :]
        return carry

    lax.fori_loop(0, rows, arrange, 0, unroll=8)
    for t in range(2):
        turned = field[1 + t].reshape(slab, 128).T
        spill[0, 1 + t] = turned[0:8]
        spill[1, 1 + t] = turned[120:128]
    pl.semaphore_wait(barrier, n - 1 + 6)

    halos = []
    for i, (sx, sz) in enumerate(SIDES):
        if sz == 0:
            src = field.at[1 if sx < 0 else 2]
            dst = field.at[3 if sx < 0 else 0]
        else:
            mine, theirs = (0, 1) if sz < 0 else (1, 0)
            if sx == 0:
                src, dst = spill.at[mine, pl.ds(1, 2)], halo_z.at[theirs, pl.ds(1, 2)]
            else:
                src = spill.at[mine, 1 if sx < 0 else 2]
                dst = halo_z.at[theirs, 3 if sx < 0 else 0]
        halos.append(pltpu.make_async_remote_copy(
            src_ref=src, dst_ref=dst, send_sem=halo_send.at[i], recv_sem=halo_recv.at[i],
            device_id=peer((sx, sz)), device_id_type=MESH))
    for copy in halos:
        copy.start()

    def send(v, i):
        to = lax.rem(me + 1 + lax.rem(i * 13, n - 1), n)
        pltpu.make_async_remote_copy(
            src_ref=obs_ref.at[v, pl.ds(pl.multiple_of(to * 32, 32), 32)],
            dst_ref=tiles.at[v, me],
            send_sem=a2a_send.at[v], recv_sem=a2a_recv.at[v],
            device_id={"xy": to}, device_id_type=MESH).start()

    lax.fori_loop(0, n - 1, lambda i, c: (send(0, i), c)[1], 0)

    def paced(group, body):
        if group is None:
            lax.fori_loop(0, STEPS, lambda i, c: (body(i), c)[1], 0)
            return
        v, half = EARLY + lax.div(group, 2), lax.rem(group, 2)
        each = n // 2
        per = each // STEPS

        def step(i, c):
            for j in range(per):
                send(v, half * each + i * per + j)
            body(i)
            return c

        lax.fori_loop(0, STEPS - 1, step, 0)
        for j in range(per - 1):
            send(v, half * each + (STEPS - 1) * per + j)

        @pl.when(half == 0)
        def _():
            send(v, each - 1)

        body(STEPS - 1)

    def taps_of(v, axis, flip):
        raw = [jnp.full((8, 128), kernels_ref[v, axis, t], F32) for t in range(TAPS)]
        whole = raw[0]
        for t in range(1, TAPS):
            whole = whole + raw[t]
        scale = 1.0 / whole
        taps = [r * scale for r in raw]
        return taps[::-1] if flip else taps

    def build(v, carry):
        raw = [kernels_ref[v, 2, t] for t in range(TAPS)]
        whole = jnp.full((1, 128), raw[0], F32)
        for t in range(1, TAPS):
            whole = whole + raw[t]
        scale = 1.0 / whole

        def banded(tap_at):
            band = jnp.zeros(tap_at.shape, F32)
            for t in range(TAPS):
                band = jnp.where(tap_at == t, raw[t], band)
            return split(band * scale)

        pair, lanes = lax.div(v, 2), pl.ds(pl.multiple_of(lax.rem(v, 2) * 128, 128), 128)
        row = lax.broadcasted_iota(jnp.int32, (128, 128), 0)
        col = lax.broadcasted_iota(jnp.int32, (128, 128), 1)
        high, low = banded(row - col + HALF)
        w_fore[pair, 0:128, lanes] = high
        w_fore[pair, 128:256, lanes] = high
        w_fore[pair, 256:384, lanes] = low
        high, low = banded(col - row + HALF)
        w_back[v, 0:128] = high
        w_back[v, 128:256] = high
        w_low[v] = low
        row = lax.broadcasted_iota(jnp.int32, (16, 128), 0)
        col = lax.broadcasted_iota(jnp.int32, (16, 128), 1)
        high, low = banded(jnp.where(row < 8, row - 8, row + 120) - col + HALF)
        w_side[v, 0:16] = high
        w_side[v, 16:32] = low
        w_fore[pair, 384:400, lanes] = high
        w_fore[pair, 400:416, lanes] = high
        w_fore[pair, 416:432, lanes] = low
        w_fore[pair, 432:512, lanes] = jnp.zeros((80, 128), BF16)
        return carry

    for copy in small:
        copy.wait()
    lax.fori_loop(0, views, build, 0)
    xed[0:8] = jnp.zeros((8, 16, 128), F32)
    xed[rows + 8:rows + 16] = jnp.zeros((8, 16, 128), F32)
    ratio[0:8] = jnp.zeros((8, 16, 128), F32)
    ratio[rows + 8:rows + 16] = jnp.zeros((8, 16, 128), F32)
    lined[0:16] = jnp.ones((16, 16, 128), F32)
    lined[rows + 16:rows + 32] = jnp.ones((16, 16, 128), F32)
    yed[:, 0:8] = jnp.zeros((rows, 8, 128), F32)
    yed[:, 24:32] = jnp.zeros((rows, 8, 128), F32)

    first, last = me == 0, me == n - 1
    front, rear = deep == 0, deep == depth - 1

    def widen(t, gone):
        high, low = split(jnp.where(gone, 0.0, field[t].reshape(slab, 128)))
        ends = []
        for side, face in ((0, front), (1, rear)):
            ends.append(jnp.where(jnp.logical_or(gone, face), 0.0, halo_z[side, t]))
        eh, el = split(jnp.concatenate(ends, axis=0))
        eh, el = eh.astype(F32), el.astype(F32)
        ends = jnp.concatenate([eh, el, eh, jnp.zeros((80, slab), F32)], axis=0).T
        wide[t, :, 0:128] = high
        wide[t, :, 128:256] = low
        wide[t, :, 256:384] = high
        wide[t, :, 384:512] = ends.astype(BF16)

    for copy in halos:
        copy.wait_recv()
    lax.fori_loop(0, n - 1, lambda i, c: (send(1, i), c)[1], 0)
    for t, gone in enumerate((first, False, False, last)):
        widen(t, gone)

    def along_y(taps, src, put, blocks):
        def block(b, carry):
            for t in range(2):
                sums = [None] * 8
                for r in range(22):
                    seen = src[b * 8 + 1 + r, pl.ds(t * 8, 8), :]
                    for j in range(max(0, r - 14), min(8, r + 1)):
                        term = taps[r - j] * seen
                        sums[j] = term if sums[j] is None else sums[j] + term
                for j in range(8):
                    put(b * 8 + j, t, sums[j])
            return carry

        lax.fori_loop(*blocks, block, 0)

    def forward(v, carry):
        part = lax.rem(v, 2)

        @pl.when(part == 0)
        def _():
            pair = lax.div(v, 2)

            for t in range(4):
                res = dot(wide[t], w_fore[pair], NN)
                for p in range(2):
                    zed[p, :, t * 8:t * 8 + 8, :] = res[:, p * 128:p * 128 + 128].reshape(rows, 8, 128)

        taps = taps_of(v, 0, False)

        def along_x(i):
            for q in range(rows // STEPS):
                y = i * (rows // STEPS) + q
                low = high = None
                for o in range(1, 24):
                    seen = zed[part, y, pl.ds(o, 8), :]
                    if o <= 15:
                        term = taps[o - 1] * seen
                        low = term if low is None else low + term
                    if o >= 9:
                        term = taps[o - 9] * seen
                        high = term if high is None else high + term
                xed[y + 8, 0:8, :] = low
                xed[y + 8, 8:16, :] = high

        paced(v, along_x)

        def put(y, t, value):
            near = pl.reciprocal(value, approx=True)
            weights[v, y, pl.ds(t * 8, 8), :] = near * (2.0 - value * near)

        along_y(taps_of(v, 1, False), xed, put, (0, rows // 8))
        return carry

    lax.fori_loop(0, views, forward, 0)

    for copy in halos:
        copy.wait_send()

    def spill_chunk(c, side):
        at = pl.ds(pl.multiple_of(c * CHUNK, CHUNK), CHUNK)
        src, dst = total.at[0 if side == 0 else 3, at], got_x.at[1 - side, at]
        return pltpu.make_async_remote_copy(
            src_ref=src, dst_ref=dst, send_sem=chunk_send.at[side, c], recv_sem=chunk_recv.at[side, c],
            device_id=peer(SIDES[side]), device_id_type=MESH)

    def backward(v, group, final):
        shift = shift_ref[v]
        whole = tiles.at[v, pl.ds(0, n - 1)]
        pltpu.make_async_copy(whole, whole, a2a_recv.at[v]).wait()
        own(v, True)

        def line(d, c):
            for p in range(2):
                for t in range(2):
                    lined[16 + d * 2 + p, pl.ds(t * 8, 8), :] = tiles[v, d, pl.ds(p + t * 16, 8, stride=2), :]
            return c

        lax.fori_loop(0, n, line, 0, unroll=4)

        def divide(y, c):
            at = y + shift
            covered = jnp.logical_and(at >= 0, at < rows)
            ratio[y + 8] = jnp.where(covered, lined[at + 16] * weights[v, y], jnp.float32(1.0))
            return c

        lax.fori_loop(0, rows, divide, 0, unroll=8)

        def put(y, t, value):
            yed[y, pl.ds(8 + t * 8, 8), :] = value

        def along_x(taps, y, to):
            sums = [None] * 4
            for o in range(1, 24):
                seen = yed[y, pl.ds(o, 8), :]
                for j in range(4):
                    t = o + 7 - 8 * j
                    if 0 <= t < TAPS:
                        term = taps[t] * seen
                        sums[j] = term if sums[j] is None else sums[j] + term
            for j in range(4):
                spread[j, to] = sums[j]

        def finish_chunk(c):
            at = pl.ds(pl.multiple_of(c * CHUNK, CHUNK), CHUNK)
            lanes = pl.ds(pl.multiple_of(c * CHUNK * 8, CHUNK * 8), CHUNK * 8)
            high, low = split(spread[:, 0:CHUNK].reshape(4 * CHUNK * 8, 128))
            res = dot(jnp.concatenate([high, low], axis=1), w_back[v], NN) + dot(high, w_low[v], NN)
            res = res.reshape(4, CHUNK, 8, 128)
            ends = dot(w_side[v], high, NT)
            ends = ends[0:16] + ends[16:32] + dot(w_side[v, 0:16], low, NT)
            for t in range(4):
                total[t, at] += res[t]
                for side in range(2):
                    spill[side, t, :, lanes] += ends[side * 8:side * 8 + 8, t * CHUNK * 8:(t + 1) * CHUNK * 8]

        def finish_tile(t):
            high, low = split(spread[t].reshape(slab, 128))
            res = dot(jnp.concatenate([high, low], axis=1), w_back[v], NN) + dot(high, w_low[v], NN)
            ends = dot(w_side[v], high, NT)
            ends = ends[0:16] + ends[16:32] + dot(w_side[v, 0:16], low, NT)
            total[t] += res.reshape(rows, 8, 128)
            for side in range(2):
                spill[side, t] += ends[side * 8:side * 8 + 8]

        if not final:
            along_y(taps_of(v, 1, True), ratio, put, (0, rows // 8))
            taps = taps_of(v, 0, True)

            def step(i):
                for q in range(rows // STEPS):
                    y = i * (rows // STEPS) + q
                    along_x(taps, y, y)

            paced(group, step)
            for t in range(4):
                finish_tile(t)
            return

        def chunk(c, k):
            along_y(taps_of(v, 1, True), ratio, put, (c * (CHUNK // 8), (c + 1) * (CHUNK // 8)))
            taps = taps_of(v, 0, True)

            def step(i, kk):
                for q in range(4):
                    along_x(taps, c * CHUNK + i * 4 + q, i * 4 + q)
                return kk

            lax.fori_loop(0, CHUNK // 4, step, 0)
            finish_chunk(c)
            for side in range(2):
                spill_chunk(c, side).start()
            return k

        lax.fori_loop(0, chunks, chunk, 0)

    for t in range(4):
        total[t] = jnp.zeros((rows, 8, 128), F32)
        spill[0, t] = jnp.zeros((8, slab), F32)
        spill[1, t] = jnp.zeros((8, slab), F32)
    with_sends = 2 * (views - EARLY) - views
    lax.fori_loop(0, with_sends, lambda v, c: (backward(v, v + views, False), c)[1], 0)
    lax.fori_loop(with_sends, views - 1, lambda v, c: (backward(v, None, False), c)[1], 0)
    backward(views - 1, None, True)

    spills = []
    for i, (sx, sz) in enumerate(SIDES[2:]):
        mine, theirs = (0, 1) if sz < 0 else (1, 0)
        if sx == 0:
            src, dst = spill.at[mine, pl.ds(1, 2)], got_z.at[theirs, pl.ds(1, 2)]
        else:
            src = spill.at[mine, 0 if sx < 0 else 3]
            dst = got_z.at[theirs, 3 if sx < 0 else 0]
        spills.append(pltpu.make_async_remote_copy(
            src_ref=src, dst_ref=dst, send_sem=spill_send.at[i], recv_sem=spill_recv.at[i],
            device_id=peer((sx, sz)), device_id_type=MESH))
    for copy in spills:
        copy.start()
    for v in range(views):
        whole = tiles.at[v, pl.ds(0, n - 1)]
        pltpu.make_async_copy(whole, whole, a2a_send.at[v]).wait()
    for copy in spills:
        copy.wait_recv()

    lane = lax.broadcasted_iota(jnp.int32, (32, 128), 1)
    row = lax.broadcasted_iota(jnp.int32, (32, 128), 0) % 16
    place = jnp.where(lane == jnp.where(row < 8, row, row + 112), 1.0, 0.0).astype(BF16)

    def last_chunk(c, k):
        at = pl.ds(pl.multiple_of(c * CHUNK, CHUNK), CHUNK)
        lanes = pl.ds(pl.multiple_of(c * CHUNK * 8, CHUNK * 8), CHUNK * 8)
        for side in range(2):
            spill_chunk(c, side).wait_recv()
        for t in range(2):
            outer, edge = (0, first) if t == 0 else (1, last)
            corner = 0 if t == 0 else 3
            ends = []
            for side, face in ((0, front), (1, rear)):
                end = got_z[side, 1 + t, :, lanes] + jnp.where(edge, 0.0, got_z[side, corner, :, lanes])
                ends.append(jnp.where(face, 0.0, end))
            both = jnp.concatenate(split(jnp.concatenate(ends, axis=0)), axis=0)
            spilled = dot(both, place, TN).reshape(CHUNK, 8, 128)
            summed = total[1 + t, at] + jnp.where(edge, 0.0, got_x[outer, at]) + spilled
            done = field[1 + t, at] * (summed * (1.0 / views))
            for q in range(CHUNK):
                out_ref[pl.ds(t * 8 * rows + c * CHUNK + q, 8, stride=rows), :] = done[q]
        return k

    lax.fori_loop(0, chunks, last_chunk, 0)
    for copy in spills:
        copy.wait_send()
    for c in range(chunks):
        for side in range(2):
            spill_chunk(c, side).wait_send()


def local(n, depth, estimate, observed, kernels, view_shift):
    views, nx = observed.shape[:2]
    rows = estimate.shape[1]
    est = estimate.reshape(16 * rows, 128)
    obs = observed.reshape(views, 2 * nx, 128)
    dma = pltpu.SemaphoreType.DMA
    vmem = lambda *shape: pltpu.VMEM(shape, F32)
    half = lambda *shape: pltpu.VMEM(shape, BF16)
    out = pl.pallas_call(
        functools.partial(kernel, n, depth, views),
        out_shape=pltpu.VMEM((16 * rows, 128), F32),
        in_specs=[
            pl.BlockSpec(memory_space=pl.ANY),
            pl.BlockSpec(memory_space=pl.ANY),
            pl.BlockSpec(memory_space=pl.ANY),
            pl.BlockSpec(memory_space=pl.ANY),
        ],
        out_specs=pl.BlockSpec(memory_space=pltpu.VMEM),
        scratch_shapes=[
            pltpu.SMEM(kernels.shape, F32),
            pltpu.SMEM((views,), jnp.int32),
            dma((2,)),
            vmem(16 * rows, 128),
            vmem(views, n, 32, 128),
            vmem(rows + 32, 16, 128),
            vmem(4, rows, 8, 128),
            half(4, rows * 8, 512),
            vmem(2, 4, 8, rows * 8),
            vmem(2, rows, 32, 128),
            vmem(rows + 16, 16, 128),
            vmem(views, rows, 16, 128),
            vmem(rows + 16, 16, 128),
            vmem(rows, 32, 128),
            vmem(4, rows, 8, 128),
            vmem(4, rows, 8, 128),
            vmem(2, 4, 8, rows * 8),
            vmem(2, rows, 8, 128),
            vmem(2, 4, 8, rows * 8),
            half(views // 2, 512, 256),
            half(views, 256, 128),
            half(views, 128, 128),
            half(views, 32, 128),
            dma(()), dma((views,)), dma((views,)), dma((views,)),
            dma((8,)), dma((8,)), dma((6,)), dma((6,)),
            dma((2, rows // CHUNK)), dma((2, rows // CHUNK)),
        ],
        compiler_params=pltpu.CompilerParams(
            collective_id=0, has_side_effects=True, vmem_limit_bytes=56 * 2**20),
    )(kernels, view_shift, est, obs)
    return out.reshape(estimate.shape)


def solution(mesh):
    return jax.shard_map(
        functools.partial(local, mesh.shape["xy"], mesh.shape["gz"]),
        mesh=mesh,
        in_specs=(P("xy", None, "gz"), P(None, None, "xy", "gz"), P(), P()),
        out_specs=P("xy", None, "gz"),
        check_vma=False,
    )
```

```python
import functools

import jax
import jax.numpy as jnp
from jax import lax
from jax.experimental import pallas as pl
from jax.experimental.pallas import tpu as pltpu
from jax.sharding import PartitionSpec as P

MESH = pl.DeviceIdType.MESH
F32, BF16 = jnp.float32, jnp.bfloat16
TAPS, HALF = 15, 7
SIDES = ((-1, 0), (1, 0), (0, -1), (0, 1), (-1, -1), (-1, 1), (1, -1), (1, 1))


def split(a):
    high = a.astype(BF16)
    return high, (a - high.astype(F32)).astype(BF16)


def dot(a, b, dims):
    return lax.dot_general(a, b, (dims, ((), ())), preferred_element_type=F32)


NN = ((1,), (0,))
NT = ((1,), (1,))
TN = ((0,), (0,))
CHUNK = 16
STEPS = 8
EARLY = 2


def kernel(n, depth, views, kernels_in, shift_in, est_ref, obs_ref, out_ref,
           kernels_ref, shift_ref, small_sem, est, tiles, lined, field, wide, halo_z, zed, xed, weights, ratio, yed, spread, total, spill,
           got_x, got_z, w_fore, w_back, w_low, w_side,
           est_sem, a2a_send, a2a_recv, own_sem, halo_send, halo_recv, spill_send, spill_recv,
           chunk_send, chunk_recv):
    rows = 2 * n
    slab = rows * 8
    chunks = rows // CHUNK
    me, deep = lax.axis_index("xy"), lax.axis_index("gz")
    def peer(side):
        return {"xy": lax.rem(me + side[0] + n, n), "gz": lax.rem(deep + side[1] + depth, depth)}

    barrier = pltpu.get_barrier_semaphore()

    def greet(k, carry):
        pl.semaphore_signal(barrier, inc=1, device_id={"xy": lax.rem(me + k, n)}, device_id_type=MESH)
        return carry

    for side in SIDES[2:]:
        pl.semaphore_signal(barrier, inc=1, device_id=peer(side), device_id_type=MESH)
    lax.fori_loop(1, n, greet, 0, unroll=31)

    load = pltpu.make_async_copy(est_ref, est, est_sem)
    load.start()
    small = (pltpu.make_async_copy(kernels_in, kernels_ref, small_sem.at[0]),
             pltpu.make_async_copy(shift_in, shift_ref, small_sem.at[1]))
    for copy in small:
        copy.start()

    def own(v, wait):
        copy = pltpu.make_async_copy(
            obs_ref.at[v, pl.ds(pl.multiple_of(me * 32, 32), 32)], tiles.at[v, me], own_sem.at[v])
        copy.wait() if wait else copy.start()

    for v in range(views):
        own(v, False)

    load.wait()

    def arrange(y, carry):
        for t in range(2):
            field[1 + t, y] = est[pl.ds(t * 8 * rows + y, 8, stride=rows), :]
        return carry

    lax.fori_loop(0, rows, arrange, 0, unroll=8)
    for t in range(2):
        turned = field[1 + t].reshape(slab, 128).T
        spill[0, 1 + t] = turned[0:8]
        spill[1, 1 + t] = turned[120:128]
    pl.semaphore_wait(barrier, n - 1 + 6)

    halos = []
    for i, (sx, sz) in enumerate(SIDES):
        if sz == 0:
            src = field.at[1 if sx < 0 else 2]
            dst = field.at[3 if sx < 0 else 0]
        else:
            mine, theirs = (0, 1) if sz < 0 else (1, 0)
            if sx == 0:
                src, dst = spill.at[mine, pl.ds(1, 2)], halo_z.at[theirs, pl.ds(1, 2)]
            else:
                src = spill.at[mine, 1 if sx < 0 else 2]
                dst = halo_z.at[theirs, 3 if sx < 0 else 0]
        halos.append(pltpu.make_async_remote_copy(
            src_ref=src, dst_ref=dst, send_sem=halo_send.at[i], recv_sem=halo_recv.at[i],
            device_id=peer((sx, sz)), device_id_type=MESH))
    for copy in halos:
        copy.start()

    def send(v, i):
        to = lax.rem(me + 1 + lax.rem(i * 13, n - 1), n)
        pltpu.make_async_remote_copy(
            src_ref=obs_ref.at[v, pl.ds(pl.multiple_of(to * 32, 32), 32)],
            dst_ref=tiles.at[v, me],
            send_sem=a2a_send.at[v], recv_sem=a2a_recv.at[v],
            device_id={"xy": to}, device_id_type=MESH).start()

    lax.fori_loop(0, n - 1, lambda i, c: (send(0, i), c)[1], 0)

    def paced(group, body):
        if group is None:
            lax.fori_loop(0, STEPS, lambda i, c: (body(i), c)[1], 0)
            return
        v, half = EARLY + lax.div(group, 2), lax.rem(group, 2)
        each = n // 2
        per = each // STEPS

        def step(i, c):
            for j in range(per):
                send(v, half * each + i * per + j)
            body(i)
            return c

        lax.fori_loop(0, STEPS - 1, step, 0)
        for j in range(per - 1):
            send(v, half * each + (STEPS - 1) * per + j)

        @pl.when(half == 0)
        def _():
            send(v, each - 1)

        body(STEPS - 1)

    def taps_of(v, axis, flip):
        raw = [jnp.full((8, 128), kernels_ref[v, axis, t], F32) for t in range(TAPS)]
        whole = raw[0]
        for t in range(1, TAPS):
            whole = whole + raw[t]
        scale = 1.0 / whole
        taps = [r * scale for r in raw]
        return taps[::-1] if flip else taps

    def build(v, carry):
        raw = [kernels_ref[v, 2, t] for t in range(TAPS)]
        whole = jnp.full((1, 128), raw[0], F32)
        for t in range(1, TAPS):
            whole = whole + raw[t]
        scale = 1.0 / whole

        def banded(tap_at):
            band = jnp.zeros(tap_at.shape, F32)
            for t in range(TAPS):
                band = jnp.where(tap_at == t, raw[t], band)
            return split(band * scale)

        pair, lanes = lax.div(v, 2), pl.ds(pl.multiple_of(lax.rem(v, 2) * 128, 128), 128)
        row = lax.broadcasted_iota(jnp.int32, (128, 128), 0)
        col = lax.broadcasted_iota(jnp.int32, (128, 128), 1)
        high, low = banded(row - col + HALF)
        w_fore[pair, 0:128, lanes] = high
        w_fore[pair, 128:256, lanes] = high
        w_fore[pair, 256:384, lanes] = low
        high, low = banded(col - row + HALF)
        w_back[v, 0:128] = high
        w_back[v, 128:256] = high
        w_low[v] = low
        row = lax.broadcasted_iota(jnp.int32, (16, 128), 0)
        col = lax.broadcasted_iota(jnp.int32, (16, 128), 1)
        high, low = banded(jnp.where(row < 8, row - 8, row + 120) - col + HALF)
        w_side[v, 0:16] = high
        w_side[v, 16:32] = low
        w_fore[pair, 384:400, lanes] = high
        w_fore[pair, 400:416, lanes] = high
        w_fore[pair, 416:432, lanes] = low
        w_fore[pair, 432:512, lanes] = jnp.zeros((80, 128), BF16)
        return carry

    for copy in small:
        copy.wait()
    lax.fori_loop(0, views, build, 0)
    xed[0:8] = jnp.zeros((8, 16, 128), F32)
    xed[rows + 8:rows + 16] = jnp.zeros((8, 16, 128), F32)
    ratio[0:8] = jnp.zeros((8, 16, 128), F32)
    ratio[rows + 8:rows + 16] = jnp.zeros((8, 16, 128), F32)
    lined[0:16] = jnp.ones((16, 16, 128), F32)
    lined[rows + 16:rows + 32] = jnp.ones((16, 16, 128), F32)
    yed[:, 0:8] = jnp.zeros((rows, 8, 128), F32)
    yed[:, 24:32] = jnp.zeros((rows, 8, 128), F32)

    first, last = me == 0, me == n - 1
    front, rear = deep == 0, deep == depth - 1

    def widen(t, gone):
        high, low = split(jnp.where(gone, 0.0, field[t].reshape(slab, 128)))
        ends = []
        for side, face in ((0, front), (1, rear)):
            ends.append(jnp.where(jnp.logical_or(gone, face), 0.0, halo_z[side, t]))
        eh, el = split(jnp.concatenate(ends, axis=0))
        eh, el = eh.astype(F32), el.astype(F32)
        ends = jnp.concatenate([eh, el, eh, jnp.zeros((80, slab), F32)], axis=0).T
        wide[t, :, 0:128] = high
        wide[t, :, 128:256] = low
        wide[t, :, 256:384] = high
        wide[t, :, 384:512] = ends.astype(BF16)

    for copy in halos:
        copy.wait_recv()
    lax.fori_loop(0, n - 1, lambda i, c: (send(1, i), c)[1], 0)
    for t, gone in enumerate((first, False, False, last)):
        widen(t, gone)

    def along_y(taps, src, put, blocks):
        def block(b, carry):
            for t in range(2):
                sums = [None] * 8
                for r in range(22):
                    seen = src[b * 8 + 1 + r, pl.ds(t * 8, 8), :]
                    for j in range(max(0, r - 14), min(8, r + 1)):
                        term = taps[r - j] * seen
                        sums[j] = term if sums[j] is None else sums[j] + term
                for j in range(8):
                    put(b * 8 + j, t, sums[j])
            return carry

        lax.fori_loop(*blocks, block, 0)

    def forward(v, carry):
        part = lax.rem(v, 2)

        @pl.when(part == 0)
        def _():
            pair = lax.div(v, 2)

            for t in range(4):
                res = dot(wide[t], w_fore[pair], NN)
                for p in range(2):
                    zed[p, :, t * 8:t * 8 + 8, :] = res[:, p * 128:p * 128 + 128].reshape(rows, 8, 128)

        taps = taps_of(v, 0, False)

        def along_x(i):
            for q in range(rows // STEPS):
                y = i * (rows // STEPS) + q
                low = high = None
                for o in range(1, 24):
                    seen = zed[part, y, pl.ds(o, 8), :]
                    if o <= 15:
                        term = taps[o - 1] * seen
                        low = term if low is None else low + term
                    if o >= 9:
                        term = taps[o - 9] * seen
                        high = term if high is None else high + term
                xed[y + 8, 0:8, :] = low
                xed[y + 8, 8:16, :] = high

        paced(v, along_x)

        def put(y, t, value):
            near = pl.reciprocal(value, approx=True)
            weights[v, y, pl.ds(t * 8, 8), :] = near * (2.0 - value * near)

        along_y(taps_of(v, 1, False), xed, put, (0, rows // 8))
        return carry

    lax.fori_loop(0, views, forward, 0)

    for copy in halos:
        copy.wait_send()

    def spill_chunk(c, side):
        at = pl.ds(pl.multiple_of(c * CHUNK, CHUNK), CHUNK)
        src, dst = total.at[0 if side == 0 else 3, at], got_x.at[1 - side, at]
        return pltpu.make_async_remote_copy(
            src_ref=src, dst_ref=dst, send_sem=chunk_send.at[side, c], recv_sem=chunk_recv.at[side, c],
            device_id=peer(SIDES[side]), device_id_type=MESH)

    spills = []
    for i, (sx, sz) in enumerate(SIDES[2:]):
        mine, theirs = (0, 1) if sz < 0 else (1, 0)
        if sx == 0:
            src, dst = spill.at[mine, pl.ds(1, 2)], got_z.at[theirs, pl.ds(1, 2)]
        else:
            src = spill.at[mine, 0 if sx < 0 else 3]
            dst = got_z.at[theirs, 3 if sx < 0 else 0]
        spills.append(pltpu.make_async_remote_copy(
            src_ref=src, dst_ref=dst, send_sem=spill_send.at[i], recv_sem=spill_recv.at[i],
            device_id=peer((sx, sz)), device_id_type=MESH))
    def backward(v, group, final):
        shift = shift_ref[v]
        whole = tiles.at[v, pl.ds(0, n - 1)]
        pltpu.make_async_copy(whole, whole, a2a_recv.at[v]).wait()
        own(v, True)

        def line(d, c):
            for p in range(2):
                for t in range(2):
                    lined[16 + d * 2 + p, pl.ds(t * 8, 8), :] = tiles[v, d, pl.ds(p + t * 16, 8, stride=2), :]
            return c

        lax.fori_loop(0, n, line, 0, unroll=4)

        def divide(y, c):
            at = y + shift
            covered = jnp.logical_and(at >= 0, at < rows)
            ratio[y + 8] = jnp.where(covered, lined[at + 16] * weights[v, y], jnp.float32(1.0))
            return c

        lax.fori_loop(0, rows, divide, 0, unroll=8)

        def put(y, t, value):
            yed[y, pl.ds(8 + t * 8, 8), :] = value

        def along_x(taps, y, to):
            sums = [None] * 4
            for o in range(1, 24):
                seen = yed[y, pl.ds(o, 8), :]
                for j in range(4):
                    t = o + 7 - 8 * j
                    if 0 <= t < TAPS:
                        term = taps[t] * seen
                        sums[j] = term if sums[j] is None else sums[j] + term
            for j in range(4):
                spread[j, to] = sums[j]

        def finish_chunk(c):
            at = pl.ds(pl.multiple_of(c * CHUNK, CHUNK), CHUNK)
            lanes = pl.ds(pl.multiple_of(c * CHUNK * 8, CHUNK * 8), CHUNK * 8)
            high, low = split(spread[:, 0:CHUNK].reshape(4 * CHUNK * 8, 128))
            res = dot(jnp.concatenate([high, low], axis=1), w_back[v], NN) + dot(high, w_low[v], NN)
            res = res.reshape(4, CHUNK, 8, 128)
            ends = dot(w_side[v], high, NT)
            ends = ends[0:16] + ends[16:32] + dot(w_side[v, 0:16], low, NT)
            for t in range(4):
                total[t, at] += res[t]
                for side in range(2):
                    spill[side, t, :, lanes] += ends[side * 8:side * 8 + 8, t * CHUNK * 8:(t + 1) * CHUNK * 8]

        def finish_tile(t):
            high, low = split(spread[t].reshape(slab, 128))
            res = dot(jnp.concatenate([high, low], axis=1), w_back[v], NN) + dot(high, w_low[v], NN)
            ends = dot(w_side[v], high, NT)
            ends = ends[0:16] + ends[16:32] + dot(w_side[v, 0:16], low, NT)
            total[t] += res.reshape(rows, 8, 128)
            for side in range(2):
                spill[side, t] += ends[side * 8:side * 8 + 8]

        if not final:
            along_y(taps_of(v, 1, True), ratio, put, (0, rows // 8))
            taps = taps_of(v, 0, True)

            def step(i):
                for q in range(rows // STEPS):
                    y = i * (rows // STEPS) + q
                    along_x(taps, y, y)

            paced(group, step)
            for t in range(4):
                finish_tile(t)
            return

        def chunk(c, k):
            along_y(taps_of(v, 1, True), ratio, put, (c * (CHUNK // 8), (c + 1) * (CHUNK // 8)))
            taps = taps_of(v, 0, True)

            def step(i, kk):
                for q in range(4):
                    along_x(taps, c * CHUNK + i * 4 + q, i * 4 + q)
                return kk

            lax.fori_loop(0, CHUNK // 4, step, 0)
            finish_chunk(c)

            @pl.when(c == chunks - 1)
            def _():
                for copy in spills:
                    copy.start()

            for side in range(2):
                spill_chunk(c, side).start()
            return k

        lax.fori_loop(0, chunks, chunk, 0)

    for t in range(4):
        total[t] = jnp.zeros((rows, 8, 128), F32)
        spill[0, t] = jnp.zeros((8, slab), F32)
        spill[1, t] = jnp.zeros((8, slab), F32)
    with_sends = 2 * (views - EARLY) - views
    lax.fori_loop(0, with_sends, lambda v, c: (backward(v, v + views, False), c)[1], 0)
    lax.fori_loop(with_sends, views - 1, lambda v, c: (backward(v, None, False), c)[1], 0)
    backward(views - 1, None, True)

    for v in range(views):
        whole = tiles.at[v, pl.ds(0, n - 1)]
        pltpu.make_async_copy(whole, whole, a2a_send.at[v]).wait()
    for copy in spills:
        copy.wait_recv()

    lane = lax.broadcasted_iota(jnp.int32, (32, 128), 1)
    row = lax.broadcasted_iota(jnp.int32, (32, 128), 0) % 16
    place = jnp.where(lane == jnp.where(row < 8, row, row + 112), 1.0, 0.0).astype(BF16)

    def last_chunk(c, k):
        at = pl.ds(pl.multiple_of(c * CHUNK, CHUNK), CHUNK)
        lanes = pl.ds(pl.multiple_of(c * CHUNK * 8, CHUNK * 8), CHUNK * 8)
        for side in range(2):
            spill_chunk(c, side).wait_recv()
        for t in range(2):
            outer, edge = (0, first) if t == 0 else (1, last)
            corner = 0 if t == 0 else 3
            ends = []
            for side, face in ((0, front), (1, rear)):
                end = got_z[side, 1 + t, :, lanes] + jnp.where(edge, 0.0, got_z[side, corner, :, lanes])
                ends.append(jnp.where(face, 0.0, end))
            both = jnp.concatenate(split(jnp.concatenate(ends, axis=0)), axis=0)
            spilled = dot(both, place, TN).reshape(CHUNK, 8, 128)
            summed = total[1 + t, at] + jnp.where(edge, 0.0, got_x[outer, at]) + spilled
            done = field[1 + t, at] * (summed * (1.0 / views))
            for q in range(CHUNK):
                out_ref[pl.ds(t * 8 * rows + c * CHUNK + q, 8, stride=rows), :] = done[q]
        return k

    lax.fori_loop(0, chunks, last_chunk, 0)
    for copy in spills:
        copy.wait_send()
    for c in range(chunks):
        for side in range(2):
            spill_chunk(c, side).wait_send()


def local(n, depth, estimate, observed, kernels, view_shift):
    views, nx = observed.shape[:2]
    rows = estimate.shape[1]
    est = estimate.reshape(16 * rows, 128)
    obs = observed.reshape(views, 2 * nx, 128)
    dma = pltpu.SemaphoreType.DMA
    vmem = lambda *shape: pltpu.VMEM(shape, F32)
    half = lambda *shape: pltpu.VMEM(shape, BF16)
    out = pl.pallas_call(
        functools.partial(kernel, n, depth, views),
        out_shape=pltpu.VMEM((16 * rows, 128), F32),
        in_specs=[
            pl.BlockSpec(memory_space=pl.ANY),
            pl.BlockSpec(memory_space=pl.ANY),
            pl.BlockSpec(memory_space=pl.ANY),
            pl.BlockSpec(memory_space=pl.ANY),
        ],
        out_specs=pl.BlockSpec(memory_space=pltpu.VMEM),
        scratch_shapes=[
            pltpu.SMEM(kernels.shape, F32),
            pltpu.SMEM((views,), jnp.int32),
            dma((2,)),
            vmem(16 * rows, 128),
            vmem(views, n, 32, 128),
            vmem(rows + 32, 16, 128),
            vmem(4, rows, 8, 128),
            half(4, rows * 8, 512),
            vmem(2, 4, 8, rows * 8),
            vmem(2, rows, 32, 128),
            vmem(rows + 16, 16, 128),
            vmem(views, rows, 16, 128),
            vmem(rows + 16, 16, 128),
            vmem(rows, 32, 128),
            vmem(4, rows, 8, 128),
            vmem(4, rows, 8, 128),
            vmem(2, 4, 8, rows * 8),
            vmem(2, rows, 8, 128),
            vmem(2, 4, 8, rows * 8),
            half(views // 2, 512, 256),
            half(views, 256, 128),
            half(views, 128, 128),
            half(views, 32, 128),
            dma(()), dma((views,)), dma((views,)), dma((views,)),
            dma((8,)), dma((8,)), dma((6,)), dma((6,)),
            dma((2, rows // CHUNK)), dma((2, rows // CHUNK)),
        ],
        compiler_params=pltpu.CompilerParams(
            collective_id=0, has_side_effects=True, vmem_limit_bytes=56 * 2**20),
    )(kernels, view_shift, est, obs)
    return out.reshape(estimate.shape)


def solution(mesh):
    return jax.shard_map(
        functools.partial(local, mesh.shape["xy"], mesh.shape["gz"]),
        mesh=mesh,
        in_specs=(P("xy", None, "gz"), P(None, None, "xy", "gz"), P(), P()),
        out_specs=P("xy", None, "gz"),
        check_vma=False,
    )
```

```python
import functools

import jax
import jax.numpy as jnp
from jax import lax
from jax.experimental import pallas as pl
from jax.experimental.pallas import tpu as pltpu
from jax.sharding import PartitionSpec as P

MESH = pl.DeviceIdType.MESH
F32, BF16 = jnp.float32, jnp.bfloat16
TAPS, HALF = 15, 7
SIDES = ((-1, 0), (1, 0), (0, -1), (0, 1), (-1, -1), (-1, 1), (1, -1), (1, 1))


def split(a):
    high = a.astype(BF16)
    return high, (a - high.astype(F32)).astype(BF16)


def dot(a, b, dims):
    return lax.dot_general(a, b, (dims, ((), ())), preferred_element_type=F32)


NN = ((1,), (0,))
NT = ((1,), (1,))
TN = ((0,), (0,))
CHUNK = 16
STEPS = 8
EARLY = 2


def kernel(n, depth, views, kernels_in, shift_in, est_ref, obs_ref, out_ref,
           kernels_ref, shift_ref, small_sem, est, tiles, lined, field, wide, halo_z, zed, xed, weights, ratio, yed, spread, total, spill,
           got_x, got_z, w_fore, w_back, w_low, w_side,
           est_sem, a2a_send, a2a_recv, own_sem, halo_send, halo_recv, spill_send, spill_recv,
           chunk_send, chunk_recv):
    rows = 2 * n
    slab = rows * 8
    chunks = rows // CHUNK
    me, deep = lax.axis_index("xy"), lax.axis_index("gz")
    def peer(side):
        return {"xy": lax.rem(me + side[0] + n, n), "gz": lax.rem(deep + side[1] + depth, depth)}

    barrier = pltpu.get_barrier_semaphore()

    def greet(k, carry):
        pl.semaphore_signal(barrier, inc=1, device_id={"xy": lax.rem(me + k, n)}, device_id_type=MESH)
        return carry

    for side in SIDES[2:]:
        pl.semaphore_signal(barrier, inc=1, device_id=peer(side), device_id_type=MESH)
    lax.fori_loop(1, n, greet, 0, unroll=31)

    load = pltpu.make_async_copy(est_ref, est, est_sem)
    load.start()
    small = (pltpu.make_async_copy(kernels_in, kernels_ref, small_sem.at[0]),
             pltpu.make_async_copy(shift_in, shift_ref, small_sem.at[1]))
    for copy in small:
        copy.start()

    def own(v, wait):
        copy = pltpu.make_async_copy(
            obs_ref.at[v, pl.ds(pl.multiple_of(me * 32, 32), 32)], tiles.at[v, me], own_sem.at[v])
        copy.wait() if wait else copy.start()

    for v in range(views):
        own(v, False)

    load.wait()

    def arrange(y, carry):
        for t in range(2):
            field[1 + t, y] = est[pl.ds(t * 8 * rows + y, 8, stride=rows), :]
        return carry

    lax.fori_loop(0, rows, arrange, 0, unroll=8)
    for t in range(2):
        turned = field[1 + t].reshape(slab, 128).T
        spill[0, 1 + t] = turned[0:8]
        spill[1, 1 + t] = turned[120:128]
    pl.semaphore_wait(barrier, n - 1 + 6)

    halos = []
    for i, (sx, sz) in enumerate(SIDES):
        if sz == 0:
            src = field.at[1 if sx < 0 else 2]
            dst = field.at[3 if sx < 0 else 0]
        else:
            mine, theirs = (0, 1) if sz < 0 else (1, 0)
            if sx == 0:
                src, dst = spill.at[mine, pl.ds(1, 2)], halo_z.at[theirs, pl.ds(1, 2)]
            else:
                src = spill.at[mine, 1 if sx < 0 else 2]
                dst = halo_z.at[theirs, 3 if sx < 0 else 0]
        halos.append(pltpu.make_async_remote_copy(
            src_ref=src, dst_ref=dst, send_sem=halo_send.at[i], recv_sem=halo_recv.at[i],
            device_id=peer((sx, sz)), device_id_type=MESH))
    for copy in halos:
        copy.start()

    def send(v, i):
        to = lax.bitwise_xor(me, 1 + lax.rem(i * 13, n - 1))
        pltpu.make_async_remote_copy(
            src_ref=obs_ref.at[v, pl.ds(pl.multiple_of(to * 32, 32), 32)],
            dst_ref=tiles.at[v, me],
            send_sem=a2a_send.at[v], recv_sem=a2a_recv.at[v],
            device_id={"xy": to}, device_id_type=MESH).start()

    lax.fori_loop(0, n - 1, lambda i, c: (send(0, i), c)[1], 0)

    def paced(group, body):
        if group is None:
            lax.fori_loop(0, STEPS, lambda i, c: (body(i), c)[1], 0)
            return
        v, half = EARLY + lax.div(group, 2), lax.rem(group, 2)
        each = n // 2
        per = each // STEPS

        def step(i, c):
            for j in range(per):
                send(v, half * each + i * per + j)
            body(i)
            return c

        lax.fori_loop(0, STEPS - 1, step, 0)
        for j in range(per - 1):
            send(v, half * each + (STEPS - 1) * per + j)

        @pl.when(half == 0)
        def _():
            send(v, each - 1)

        body(STEPS - 1)

    def taps_of(v, axis, flip):
        raw = [jnp.full((8, 128), kernels_ref[v, axis, t], F32) for t in range(TAPS)]
        whole = raw[0]
        for t in range(1, TAPS):
            whole = whole + raw[t]
        scale = 1.0 / whole
        taps = [r * scale for r in raw]
        return taps[::-1] if flip else taps

    def build(v, carry):
        raw = [kernels_ref[v, 2, t] for t in range(TAPS)]
        whole = jnp.full((1, 128), raw[0], F32)
        for t in range(1, TAPS):
            whole = whole + raw[t]
        scale = 1.0 / whole

        def banded(tap_at):
            band = jnp.zeros(tap_at.shape, F32)
            for t in range(TAPS):
                band = jnp.where(tap_at == t, raw[t], band)
            return split(band * scale)

        pair, lanes = lax.div(v, 2), pl.ds(pl.multiple_of(lax.rem(v, 2) * 128, 128), 128)
        row = lax.broadcasted_iota(jnp.int32, (128, 128), 0)
        col = lax.broadcasted_iota(jnp.int32, (128, 128), 1)
        high, low = banded(row - col + HALF)
        w_fore[pair, 0:128, lanes] = high
        w_fore[pair, 128:256, lanes] = high
        w_fore[pair, 256:384, lanes] = low
        high, low = banded(col - row + HALF)
        w_back[v, 0:128] = high
        w_back[v, 128:256] = high
        w_low[v] = low
        row = lax.broadcasted_iota(jnp.int32, (16, 128), 0)
        col = lax.broadcasted_iota(jnp.int32, (16, 128), 1)
        high, low = banded(jnp.where(row < 8, row - 8, row + 120) - col + HALF)
        w_side[v, 0:16] = high
        w_side[v, 16:32] = low
        w_fore[pair, 384:400, lanes] = high
        w_fore[pair, 400:416, lanes] = high
        w_fore[pair, 416:432, lanes] = low
        w_fore[pair, 432:512, lanes] = jnp.zeros((80, 128), BF16)
        return carry

    for copy in small:
        copy.wait()
    lax.fori_loop(0, views, build, 0)
    xed[0:8] = jnp.zeros((8, 16, 128), F32)
    xed[rows + 8:rows + 16] = jnp.zeros((8, 16, 128), F32)
    ratio[0:8] = jnp.zeros((8, 16, 128), F32)
    ratio[rows + 8:rows + 16] = jnp.zeros((8, 16, 128), F32)
    lined[0:16] = jnp.ones((16, 16, 128), F32)
    lined[rows + 16:rows + 32] = jnp.ones((16, 16, 128), F32)
    yed[:, 0:8] = jnp.zeros((rows, 8, 128), F32)
    yed[:, 24:32] = jnp.zeros((rows, 8, 128), F32)

    first, last = me == 0, me == n - 1
    front, rear = deep == 0, deep == depth - 1

    def widen(t, gone):
        high, low = split(jnp.where(gone, 0.0, field[t].reshape(slab, 128)))
        ends = []
        for side, face in ((0, front), (1, rear)):
            ends.append(jnp.where(jnp.logical_or(gone, face), 0.0, halo_z[side, t]))
        eh, el = split(jnp.concatenate(ends, axis=0))
        eh, el = eh.astype(F32), el.astype(F32)
        ends = jnp.concatenate([eh, el, eh, jnp.zeros((80, slab), F32)], axis=0).T
        wide[t, :, 0:128] = high
        wide[t, :, 128:256] = low
        wide[t, :, 256:384] = high
        wide[t, :, 384:512] = ends.astype(BF16)

    for copy in halos:
        copy.wait_recv()
    lax.fori_loop(0, n - 1, lambda i, c: (send(1, i), c)[1], 0)
    for t, gone in enumerate((first, False, False, last)):
        widen(t, gone)

    def along_y(taps, src, put, blocks):
        def block(b, carry):
            for t in range(2):
                sums = [None] * 8
                for r in range(22):
                    seen = src[b * 8 + 1 + r, pl.ds(t * 8, 8), :]
                    for j in range(max(0, r - 14), min(8, r + 1)):
                        term = taps[r - j] * seen
                        sums[j] = term if sums[j] is None else sums[j] + term
                for j in range(8):
                    put(b * 8 + j, t, sums[j])
            return carry

        lax.fori_loop(*blocks, block, 0)

    def forward(v, carry):
        part = lax.rem(v, 2)

        @pl.when(part == 0)
        def _():
            pair = lax.div(v, 2)

            for t in range(4):
                res = dot(wide[t], w_fore[pair], NN)
                for p in range(2):
                    zed[p, :, t * 8:t * 8 + 8, :] = res[:, p * 128:p * 128 + 128].reshape(rows, 8, 128)

        taps = taps_of(v, 0, False)

        def along_x(i):
            for q in range(rows // STEPS):
                y = i * (rows // STEPS) + q
                low = high = None
                for o in range(1, 24):
                    seen = zed[part, y, pl.ds(o, 8), :]
                    if o <= 15:
                        term = taps[o - 1] * seen
                        low = term if low is None else low + term
                    if o >= 9:
                        term = taps[o - 9] * seen
                        high = term if high is None else high + term
                xed[y + 8, 0:8, :] = low
                xed[y + 8, 8:16, :] = high

        paced(v, along_x)

        def put(y, t, value):
            near = pl.reciprocal(value, approx=True)
            weights[v, y, pl.ds(t * 8, 8), :] = near * (2.0 - value * near)

        along_y(taps_of(v, 1, False), xed, put, (0, rows // 8))
        return carry

    lax.fori_loop(0, views, forward, 0)

    for copy in halos:
        copy.wait_send()

    def spill_chunk(c, side):
        at = pl.ds(pl.multiple_of(c * CHUNK, CHUNK), CHUNK)
        src, dst = total.at[0 if side == 0 else 3, at], got_x.at[1 - side, at]
        return pltpu.make_async_remote_copy(
            src_ref=src, dst_ref=dst, send_sem=chunk_send.at[side, c], recv_sem=chunk_recv.at[side, c],
            device_id=peer(SIDES[side]), device_id_type=MESH)

    spills = []
    for i, (sx, sz) in enumerate(SIDES[2:]):
        mine, theirs = (0, 1) if sz < 0 else (1, 0)
        if sx == 0:
            src, dst = spill.at[mine, pl.ds(1, 2)], got_z.at[theirs, pl.ds(1, 2)]
        else:
            src = spill.at[mine, 0 if sx < 0 else 3]
            dst = got_z.at[theirs, 3 if sx < 0 else 0]
        spills.append(pltpu.make_async_remote_copy(
            src_ref=src, dst_ref=dst, send_sem=spill_send.at[i], recv_sem=spill_recv.at[i],
            device_id=peer((sx, sz)), device_id_type=MESH))
    def backward(v, group, final):
        shift = shift_ref[v]
        whole = tiles.at[v, pl.ds(0, n - 1)]
        pltpu.make_async_copy(whole, whole, a2a_recv.at[v]).wait()
        own(v, True)

        def line(d, c):
            for p in range(2):
                for t in range(2):
                    lined[16 + d * 2 + p, pl.ds(t * 8, 8), :] = tiles[v, d, pl.ds(p + t * 16, 8, stride=2), :]
            return c

        lax.fori_loop(0, n, line, 0, unroll=4)

        def divide(y, c):
            at = y + shift
            covered = jnp.logical_and(at >= 0, at < rows)
            ratio[y + 8] = jnp.where(covered, lined[at + 16] * weights[v, y], jnp.float32(1.0))
            return c

        lax.fori_loop(0, rows, divide, 0, unroll=8)

        def put(y, t, value):
            yed[y, pl.ds(8 + t * 8, 8), :] = value

        def along_x(taps, y, to):
            sums = [None] * 4
            for o in range(1, 24):
                seen = yed[y, pl.ds(o, 8), :]
                for j in range(4):
                    t = o + 7 - 8 * j
                    if 0 <= t < TAPS:
                        term = taps[t] * seen
                        sums[j] = term if sums[j] is None else sums[j] + term
            for j in range(4):
                spread[j, to] = sums[j]

        def finish_chunk(c):
            at = pl.ds(pl.multiple_of(c * CHUNK, CHUNK), CHUNK)
            lanes = pl.ds(pl.multiple_of(c * CHUNK * 8, CHUNK * 8), CHUNK * 8)
            high, low = split(spread[:, 0:CHUNK].reshape(4 * CHUNK * 8, 128))
            res = dot(jnp.concatenate([high, low], axis=1), w_back[v], NN) + dot(high, w_low[v], NN)
            res = res.reshape(4, CHUNK, 8, 128)
            ends = dot(w_side[v], high, NT)
            ends = ends[0:16] + ends[16:32] + dot(w_side[v, 0:16], low, NT)
            for t in range(4):
                total[t, at] += res[t]
                for side in range(2):
                    spill[side, t, :, lanes] += ends[side * 8:side * 8 + 8, t * CHUNK * 8:(t + 1) * CHUNK * 8]

        def finish_tile(t):
            high, low = split(spread[t].reshape(slab, 128))
            res = dot(jnp.concatenate([high, low], axis=1), w_back[v], NN) + dot(high, w_low[v], NN)
            ends = dot(w_side[v], high, NT)
            ends = ends[0:16] + ends[16:32] + dot(w_side[v, 0:16], low, NT)
            total[t] += res.reshape(rows, 8, 128)
            for side in range(2):
                spill[side, t] += ends[side * 8:side * 8 + 8]

        if not final:
            along_y(taps_of(v, 1, True), ratio, put, (0, rows // 8))
            taps = taps_of(v, 0, True)

            def step(i):
                for q in range(rows // STEPS):
                    y = i * (rows // STEPS) + q
                    along_x(taps, y, y)

            paced(group, step)
            for t in range(4):
                finish_tile(t)
            return

        def chunk(c, k):
            along_y(taps_of(v, 1, True), ratio, put, (c * (CHUNK // 8), (c + 1) * (CHUNK // 8)))
            taps = taps_of(v, 0, True)

            def step(i, kk):
                for q in range(4):
                    along_x(taps, c * CHUNK + i * 4 + q, i * 4 + q)
                return kk

            lax.fori_loop(0, CHUNK // 4, step, 0)
            finish_chunk(c)

            @pl.when(c == chunks - 1)
            def _():
                for copy in spills:
                    copy.start()

            for side in range(2):
                spill_chunk(c, side).start()
            return k

        lax.fori_loop(0, chunks, chunk, 0)

    for t in range(4):
        total[t] = jnp.zeros((rows, 8, 128), F32)
        spill[0, t] = jnp.zeros((8, slab), F32)
        spill[1, t] = jnp.zeros((8, slab), F32)
    with_sends = 2 * (views - EARLY) - views
    lax.fori_loop(0, with_sends, lambda v, c: (backward(v, v + views, False), c)[1], 0)
    lax.fori_loop(with_sends, views - 1, lambda v, c: (backward(v, None, False), c)[1], 0)
    backward(views - 1, None, True)

    for v in range(views):
        whole = tiles.at[v, pl.ds(0, n - 1)]
        pltpu.make_async_copy(whole, whole, a2a_send.at[v]).wait()
    for copy in spills:
        copy.wait_recv()

    lane = lax.broadcasted_iota(jnp.int32, (32, 128), 1)
    row = lax.broadcasted_iota(jnp.int32, (32, 128), 0) % 16
    place = jnp.where(lane == jnp.where(row < 8, row, row + 112), 1.0, 0.0).astype(BF16)

    def last_chunk(c, k):
        at = pl.ds(pl.multiple_of(c * CHUNK, CHUNK), CHUNK)
        lanes = pl.ds(pl.multiple_of(c * CHUNK * 8, CHUNK * 8), CHUNK * 8)
        for side in range(2):
            spill_chunk(c, side).wait_recv()
        for t in range(2):
            outer, edge = (0, first) if t == 0 else (1, last)
            corner = 0 if t == 0 else 3
            ends = []
            for side, face in ((0, front), (1, rear)):
                end = got_z[side, 1 + t, :, lanes] + jnp.where(edge, 0.0, got_z[side, corner, :, lanes])
                ends.append(jnp.where(face, 0.0, end))
            both = jnp.concatenate(split(jnp.concatenate(ends, axis=0)), axis=0)
            spilled = dot(both, place, TN).reshape(CHUNK, 8, 128)
            summed = total[1 + t, at] + jnp.where(edge, 0.0, got_x[outer, at]) + spilled
            done = field[1 + t, at] * (summed * (1.0 / views))
            for q in range(CHUNK):
                out_ref[pl.ds(t * 8 * rows + c * CHUNK + q, 8, stride=rows), :] = done[q]
        return k

    lax.fori_loop(0, chunks, last_chunk, 0)
    for copy in spills:
        copy.wait_send()
    for c in range(chunks):
        for side in range(2):
            spill_chunk(c, side).wait_send()


def local(n, depth, estimate, observed, kernels, view_shift):
    views, nx = observed.shape[:2]
    rows = estimate.shape[1]
    est = estimate.reshape(16 * rows, 128)
    obs = observed.reshape(views, 2 * nx, 128)
    dma = pltpu.SemaphoreType.DMA
    vmem = lambda *shape: pltpu.VMEM(shape, F32)
    half = lambda *shape: pltpu.VMEM(shape, BF16)
    out = pl.pallas_call(
        functools.partial(kernel, n, depth, views),
        out_shape=pltpu.VMEM((16 * rows, 128), F32),
        in_specs=[
            pl.BlockSpec(memory_space=pl.ANY),
            pl.BlockSpec(memory_space=pl.ANY),
            pl.BlockSpec(memory_space=pl.ANY),
            pl.BlockSpec(memory_space=pl.ANY),
        ],
        out_specs=pl.BlockSpec(memory_space=pltpu.VMEM),
        scratch_shapes=[
            pltpu.SMEM(kernels.shape, F32),
            pltpu.SMEM((views,), jnp.int32),
            dma((2,)),
            vmem(16 * rows, 128),
            vmem(views, n, 32, 128),
            vmem(rows + 32, 16, 128),
            vmem(4, rows, 8, 128),
            half(4, rows * 8, 512),
            vmem(2, 4, 8, rows * 8),
            vmem(2, rows, 32, 128),
            vmem(rows + 16, 16, 128),
            vmem(views, rows, 16, 128),
            vmem(rows + 16, 16, 128),
            vmem(rows, 32, 128),
            vmem(4, rows, 8, 128),
            vmem(4, rows, 8, 128),
            vmem(2, 4, 8, rows * 8),
            vmem(2, rows, 8, 128),
            vmem(2, 4, 8, rows * 8),
            half(views // 2, 512, 256),
            half(views, 256, 128),
            half(views, 128, 128),
            half(views, 32, 128),
            dma(()), dma((views,)), dma((views,)), dma((views,)),
            dma((8,)), dma((8,)), dma((6,)), dma((6,)),
            dma((2, rows // CHUNK)), dma((2, rows // CHUNK)),
        ],
        compiler_params=pltpu.CompilerParams(
            collective_id=0, has_side_effects=True, vmem_limit_bytes=56 * 2**20),
    )(kernels, view_shift, est, obs)
    return out.reshape(estimate.shape)


def solution(mesh):
    return jax.shard_map(
        functools.partial(local, mesh.shape["xy"], mesh.shape["gz"]),
        mesh=mesh,
        in_specs=(P("xy", None, "gz"), P(None, None, "xy", "gz"), P(), P()),
        out_specs=P("xy", None, "gz"),
        check_vma=False,
    )
```
